512 devices in a mesh: img: 16 (over z_lo, core), txt: 32 (over y, z_hi, x).
Axes of the slice: x: 4, y: 4, z: 16 (z_hi: 2, z_lo: 8; z = z_hi * 8 + z_lo), core: 2. Of those that a mesh axis runs over, the one named last changes fastest.
Arguments:
- image_feats: bfloat16 [8192, 768], P(('img', 'txt')), may hold values from -6 to 6
- text_feats: bfloat16 [8192, 512], P(('txt', 'img')), may hold values from -6 to 6
- teacher_img: bfloat16 [8192, 1024], P(('img', 'txt')), may hold values from -60 to 60, as said below
- teacher_txt: bfloat16 [8192, 1024], P(('txt', 'img')), may hold values from -60 to 60, as said below
- proj_img: bfloat16 [768, 512], replicated, may hold values from -0.21875 to 0.21875
- proj_txt: bfloat16 [512, 512], replicated, may hold values from -0.25 to 0.25
Outputs:
- loss: float32 [], replicated
- grad_img: float32 [768, 512], replicated
- grad_txt: float32 [512, 512], replicated
The draws below stay inside these ranges and needn't reach their ends.
Inputs may be any that keep to these rules, and one draw needn't show every extreme that they name: `teacher_img`: raw teacher embeddings, rows of various scales. `teacher_txt`: raw teacher embeddings, rows of various scales.
All inputs are finite; a program needn't handle non-finite values.
Results may differ from the reference program's by a relative error of at most 0.0077.
Values may be sent and summed in bfloat16 or wider, within the bound.
No kernel may reach another device: no remote copies, remote signals or barrier semaphores. Data moves between devices by JAX's collectives and lax.ppermute only.
A program may use at most 64 MiB of HBM per device.

```python
import jax
import jax.numpy as jnp
from jax import lax

DT = 1024
DS = 512
FI = 768
FT = 512
BATCH = 8192


def teacher_rows(key, own_key):
    scale_key = jax.random.fold_in(own_key, 5)
    scales = jnp.exp(jax.random.uniform(scale_key, (BATCH, 1), jnp.float32, 0.0, jnp.log(10.0)))
    own = jax.random.truncated_normal(own_key, -4.0, 4.0, (BATCH, DT), jnp.float32)
    return (own * scales).astype(jnp.bfloat16)


def draw_teacher_img(key, part):
    own_key = jax.random.fold_in(key, 11)
    return teacher_rows(key, own_key)


def draw_teacher_txt(key, part):
    own_key = jax.random.fold_in(key, 12)
    return teacher_rows(key, own_key)


def level_of(rng, extent, pieces, least, largest):
    gain = 1.0
    for axis_at, blocks in pieces:
        steps = jax.random.uniform(jax.random.fold_in(jax.random.fold_in(rng, 6), axis_at), (blocks,), jnp.float32, least / len(pieces), largest / len(pieces))
        gain = gain * jnp.repeat(jnp.exp(steps), extent[axis_at] // blocks).reshape((-1,) + (1,) * (len(extent) - 1 - axis_at))
    return gain


def noise(key, shape, scale, bound, split=(), kind=jnp.bfloat16):
    values = jax.random.normal(key, shape, jnp.float32) * scale
    if len(split) > 0:
        values = level_of(key, shape, split, -0.22, 0.18) * values
    return jnp.clip(values, min=-bound, max=bound).astype(kind)


def setup_inputs(seed: int = 0) -> dict:
    streams_of = jax.random.split(jax.random.key(seed), 7)
    return {
        "image_feats": noise(streams_of[0], (BATCH, FI), 1.0, 6.0, ((0, 512),)),
        "text_feats": noise(streams_of[1], (BATCH, FT), 1.0, 6.0, ((0, 512),)),
        "teacher_img": draw_teacher_img(jax.random.fold_in(streams_of[6], 71), 0),
        "teacher_txt": draw_teacher_txt(jax.random.fold_in(streams_of[6], 71), 0),
        "proj_img": noise(streams_of[4], (FI, DS), FI ** -0.5, 0.21875),
        "proj_txt": noise(streams_of[5], (FT, DS), FT ** -0.5, 0.25),
    }


EPS = 1e-06
TEACHER_SCALE = 100.0
STUDENT_SCALE = 50.0

def project(feats, weight):
    u = jnp.dot(feats, weight, preferred_element_type=jnp.float32)
    inv = lax.rsqrt(lax.optimization_barrier(jnp.sum(u * u, axis=1, keepdims=True)) + EPS)
    return (u * inv, inv)

def normed(raw):
    x = raw.astype(jnp.float32)
    return (x * lax.rsqrt(lax.optimization_barrier(jnp.sum(x * x, axis=1, keepdims=True)) + EPS)).astype(jnp.bfloat16)

def reference(image_feats, text_feats, teacher_img, teacher_txt, proj_img, proj_txt):
    e_img, inv_img = project(image_feats, proj_img)
    e_txt, inv_txt = project(text_feats, proj_txt)
    s_img = e_img.astype(jnp.bfloat16)
    s_txt = e_txt.astype(jnp.bfloat16)
    q_img = normed(teacher_img)
    q_txt = normed(teacher_txt)
    block = min(1024, BATCH)
    count = BATCH // block

    def tiles(k):
        start = (k * block).astype(jnp.int32)
        qb = lax.dynamic_slice_in_dim(q_img, start, block, 0)
        sb = lax.dynamic_slice_in_dim(s_img, start, block, 0)
        tl = TEACHER_SCALE * jnp.dot(qb, q_txt.T, preferred_element_type=jnp.float32)
        sl = STUDENT_SCALE * jnp.dot(sb, s_txt.T, preferred_element_type=jnp.float32)
        return (tl, sl, sb)

    def col_step(carry, k):
        tm, ts, sm, ss = carry
        tl, sl, sb = tiles(k)
        tm2 = jnp.maximum(tm, tl.max(0))
        sm2 = jnp.maximum(sm, sl.max(0))
        ts2 = ts * jnp.exp(tm - tm2) + lax.optimization_barrier(jnp.sum(jnp.exp(tl - tm2[None, :]), 0))
        ss2 = ss * jnp.exp(sm - sm2) + lax.optimization_barrier(jnp.sum(jnp.exp(sl - sm2[None, :]), 0))
        return ((tm2, ts2, sm2, ss2), None)
    low = jnp.full((BATCH,), -jnp.inf, jnp.float32)
    zero = jnp.zeros((BATCH,), jnp.float32)
    (ctm, cts, csm, css), _ = lax.scan(col_step, (low, zero, low, zero), jnp.arange(count, dtype=jnp.int32))

    def grad_step(carry, k):
        acc_txt, total = carry
        tl, sl, sb = tiles(k)
        rtm = tl.max(1)
        rsm = sl.max(1)
        et_row = jnp.exp(tl - rtm[:, None])
        es_row = jnp.exp(sl - rsm[:, None])
        rts = lax.optimization_barrier(jnp.sum(et_row, 1))
        rss = lax.optimization_barrier(jnp.sum(es_row, 1))
        pt_row = et_row / rts[:, None]
        ps_row = es_row / rss[:, None]
        pt_col = jnp.exp(tl - ctm[None, :]) / cts[None, :]
        ps_col = jnp.exp(sl - csm[None, :]) / css[None, :]
        diff = tl - sl
        term = jnp.sum(pt_row * diff) + jnp.sum(pt_col * diff)
        term = term + jnp.sum(rsm + jnp.log(rss) - rtm - jnp.log(rts))
        grad_tile = (0.5 * STUDENT_SCALE * (ps_row - pt_row + (ps_col - pt_col))).astype(jnp.bfloat16)
        d_img = jnp.dot(grad_tile, s_txt, preferred_element_type=jnp.float32)
        acc_txt = acc_txt + lax.dot_general(grad_tile, sb, (((0,), (0,)), ((), ())), preferred_element_type=jnp.float32)
        return ((acc_txt, total + term), d_img)
    init = (jnp.zeros((BATCH, DS), jnp.float32), jnp.zeros((), jnp.float32))
    (d_txt, total), d_blocks = lax.scan(grad_step, init, jnp.arange(count, dtype=jnp.int32))
    d_img = d_blocks.reshape(BATCH, DS)
    total = total + jnp.sum(csm + jnp.log(css) - ctm - jnp.log(cts))
    du_img = (d_img - e_img * lax.optimization_barrier(jnp.sum(e_img * d_img, 1, keepdims=True))) * inv_img
    du_txt = (d_txt - e_txt * lax.optimization_barrier(jnp.sum(e_txt * d_txt, 1, keepdims=True))) * inv_txt
    grad_img = jnp.dot(image_feats.astype(jnp.float32).T, du_img, precision=lax.Precision.HIGHEST)
    grad_txt = jnp.dot(text_feats.astype(jnp.float32).T, du_txt, precision=lax.Precision.HIGHEST)
    loss = total / (2.0 * BATCH)
    return (loss, grad_img, grad_txt)
```

```python
import jax
import jax.numpy as jnp
from jax import lax
from jax.sharding import Mesh
from jax.sharding import PartitionSpec as P

EPS = 1e-06
TEACHER_SCALE = 100.0
STUDENT_SCALE = 50.0

AXES = ("zl", "core", "y", "zh", "x")
SIZES = (8, 2, 4, 2, 4)
PLANE = ("y", "x")
RING = ("zh", "zl")
TILE = ("core", "y", "x")

BF16 = jnp.bfloat16
F32 = jnp.float32


def project(feats, weight):
    u = jnp.dot(feats, weight, preferred_element_type=F32)
    inv = lax.rsqrt(jnp.sum(u * u, axis=1, keepdims=True) + EPS)
    return (u * inv, inv)


def normed(raw):
    x = raw.astype(F32)
    return (x * lax.rsqrt(jnp.sum(x * x, axis=1, keepdims=True) + EPS)).astype(BF16)


def tangent(grad_rows, embeds, inverse):
    return (grad_rows - embeds * jnp.sum(embeds * grad_rows, 1, keepdims=True)) * inverse


def spread(block, axes):
    count = lax.axis_size(axes)
    copies = jnp.broadcast_to(block[None], (count,) + block.shape)
    return lax.all_to_all(copies, axes, 0, 0, tiled=True)


def swap_cores(block):
    return lax.ppermute(block, "core", [(0, 1), (1, 0)])


def thirds(value):
    hi = value.astype(BF16)
    rest = value - hi.astype(F32)
    mid = rest.astype(BF16)
    low = (rest - mid.astype(F32)).astype(BF16)
    return jnp.stack([hi, mid, low])


def with_loss(rows, value):
    extra = jnp.zeros((8, rows.shape[1]), BF16)
    extra = extra.at[0, :3].set(thirds(value))
    return jnp.concatenate([rows.astype(BF16), extra], 0)


def merge(stats):
    top = jnp.max(stats[:, 0], 0)
    teacher = jnp.sum(stats[:, 1] * jnp.exp(stats[:, 0] - top[None]), 0)
    student = jnp.sum(stats[:, 2], 0)
    return (top, teacher, student)


def shards(image_feats, text_feats, teacher_img, teacher_txt, proj_img, proj_txt):
    core = lax.axis_index("core")
    dt = teacher_img.shape[1]
    pack_img = jnp.concatenate([normed(teacher_img), image_feats], 1)
    pack_txt = jnp.concatenate([normed(teacher_txt), text_feats], 1)
    half_img = spread(pack_img, PLANE)
    half_img = half_img.reshape(-1, pack_img.shape[1])
    half_img, pack_txt = lax.optimization_barrier((half_img, pack_txt))
    other_img = swap_cores(half_img)
    block_txt = lax.all_gather(pack_txt, RING, axis=0, tiled=True)
    block_img = jnp.concatenate([half_img, other_img], 0)
    q_img, feats_img = (block_img[:, :dt], block_img[:, dt:])
    q_txt, feats_txt = (block_txt[:, :dt], block_txt[:, dt:])
    e_img, inv_img = project(feats_img, proj_img)
    e_txt, inv_txt = project(feats_txt, proj_txt)
    s_img = e_img.astype(BF16)
    s_txt = e_txt.astype(BF16)
    rows, cols = (q_img.shape[0], q_txt.shape[0])

    tl = TEACHER_SCALE * jnp.dot(q_img, q_txt.T, preferred_element_type=F32)
    sl = STUDENT_SCALE * jnp.dot(s_img, s_txt.T, preferred_element_type=F32)
    rm = tl.max(1)
    cm = tl.max(0)
    er = jnp.exp(tl - rm[:, None])
    ec = jnp.exp(tl - cm[None, :])
    es = jnp.exp(sl)
    row_stats = jnp.stack([rm, er.sum(1), es.sum(1)]).reshape(3, 2, -1)
    col_stats = jnp.stack([cm, ec.sum(0), es.sum(0)])
    row_stats = jnp.where(core == 0, row_stats, row_stats[:, ::-1])
    row_all = spread(row_stats.reshape(-1, 128), TILE).reshape(-1, 3, rows)
    row_all, col_stats = lax.optimization_barrier((row_all, col_stats))
    col_all = spread(col_stats.reshape(-1, 128), RING).reshape(-1, 3, cols)
    row_top, row_t, row_s = merge(row_all)
    col_top, col_t, col_s = merge(col_all)
    row_lse = jnp.sum(jnp.log(row_s) - row_top - jnp.log(row_t))
    col_lse = jnp.sum(jnp.log(col_s) - col_top - jnp.log(col_t))
    mine = jnp.stack([row_top, 1.0 / row_t, 1.0 / row_s]).reshape(3, 2, -1)
    mine = jnp.where(core == 0, mine, mine[:, ::-1]).reshape(3, rows)
    row_gain = jnp.exp(rm - mine[0]) * mine[1]
    col_gain = jnp.exp(cm - col_top) / col_t
    pt = er * row_gain[:, None] + ec * col_gain[None, :]
    ps = es * mine[2][:, None] + es * (1.0 / col_s)[None, :]
    total = jnp.sum(pt * (tl - sl))
    total = total + row_lse / lax.axis_size(TILE) + col_lse / lax.axis_size(RING)
    g = (0.5 * STUDENT_SCALE * (ps - pt)).astype(BF16)
    d_img = jnp.dot(g, s_txt, preferred_element_type=F32)
    d_txt = lax.dot_general(g, s_img, (((0,), (0,)), ((), ())), preferred_element_type=F32)
    du_img = tangent(d_img, e_img, inv_img).astype(BF16)
    du_txt = tangent(d_txt, e_txt, inv_txt).astype(BF16)
    rows_first = (((0,), (0,)), ((), ()))
    w_img = lax.dot_general(feats_img, du_img, rows_first, preferred_element_type=F32)
    w_txt = lax.dot_general(feats_txt, du_txt, rows_first, preferred_element_type=F32)
    part = jnp.concatenate([w_img.astype(BF16), w_txt.astype(BF16)], 0)

    width = part.shape[1]
    part = part.reshape(2, -1, width)
    part = lax.all_to_all(part, "core", 0, 0, tiled=True).astype(F32).sum(0).astype(BF16)
    part = part.reshape(lax.axis_size(PLANE), -1, width)
    part = lax.all_to_all(part, PLANE, 0, 0, tiled=True).astype(F32).sum(0)
    chunk = part.shape[0]
    part = lax.all_gather(with_loss(part, total), RING).astype(F32)
    chunk_sum = part[:, :chunk].sum(0)
    ring_loss = part[:, chunk, :3].sum()
    full = spread(with_loss(chunk_sum, ring_loss), PLANE)
    full = spread(full, "core").astype(F32)
    full = full.reshape(-1, chunk + 8, width)
    grads = full[:, :chunk].reshape(-1, width)
    batch_total = image_feats.shape[0] * lax.axis_size(AXES)
    loss = full[:, chunk, :3].sum() / (2.0 * batch_total)
    split = image_feats.shape[1]
    return (loss, grads[:split], grads[split:])


def solution(mesh):
    fine = Mesh(mesh.devices.reshape(SIZES), AXES)
    img = P(("zl", "core", "y", "zh", "x"), None)
    txt = P(("y", "zh", "x", "zl", "core"), None)
    return jax.shard_map(
        shards,
        mesh=fine,
        in_specs=(img, txt, img, txt, P(), P()),
        out_specs=(P(), P(), P()),
        check_vma=False,
    )
```

```python
import jax
import jax.numpy as jnp
from jax import lax
from jax.sharding import Mesh
from jax.sharding import PartitionSpec as P

EPS = 1e-06
TEACHER_SCALE = 100.0
STUDENT_SCALE = 50.0

AXES = ("zl", "core", "y", "zh", "x")
SIZES = (8, 2, 4, 2, 4)
PLANE = ("y", "x")
RING = ("zh", "zl")
TILE = ("core", "y", "x")

BF16 = jnp.bfloat16
F32 = jnp.float32


def project(feats, weight):
    u = jnp.dot(feats, weight, preferred_element_type=F32)
    inv = lax.rsqrt(jnp.sum(u * u, axis=1, keepdims=True) + EPS)
    return (u * inv, inv)


def normed(raw):
    x = raw.astype(F32)
    return (x * lax.rsqrt(jnp.sum(x * x, axis=1, keepdims=True) + EPS)).astype(BF16)


def tangent(grad_rows, embeds, inverse):
    return (grad_rows - embeds * jnp.sum(embeds * grad_rows, 1, keepdims=True)) * inverse


def spread(block, axes):
    count = lax.axis_size(axes)
    copies = jnp.broadcast_to(block[None], (count,) + block.shape)
    return lax.all_to_all(copies, axes, 0, 0, tiled=True)


def swap_cores(block):
    return lax.ppermute(block, "core", [(0, 1), (1, 0)])


def thirds(value):
    hi = value.astype(BF16)
    rest = value - hi.astype(F32)
    mid = rest.astype(BF16)
    low = (rest - mid.astype(F32)).astype(BF16)
    return jnp.stack([hi, mid, low])


def with_loss(rows, value):
    extra = jnp.zeros((8, rows.shape[1]), BF16)
    extra = extra.at[0, :3].set(thirds(value))
    return jnp.concatenate([rows.astype(BF16), extra], 0)


def merge(stats):
    top = jnp.max(stats[:, 0], 0)
    teacher = jnp.sum(stats[:, 1] * jnp.exp(stats[:, 0] - top[None]), 0)
    student = jnp.sum(stats[:, 2], 0)
    return (top, teacher, student)


def shards(image_feats, text_feats, teacher_img, teacher_txt, proj_img, proj_txt):
    core = lax.axis_index("core")
    dt = teacher_img.shape[1]
    pack_img = jnp.concatenate([normed(teacher_img), image_feats], 1)
    pack_txt = jnp.concatenate([normed(teacher_txt), text_feats], 1)
    half_img = spread(pack_img, PLANE)
    half_img = half_img.reshape(-1, pack_img.shape[1])
    other_img = swap_cores(half_img)
    block_txt = lax.all_gather(pack_txt, RING, axis=0, tiled=True)
    block_img = jnp.concatenate([half_img, other_img], 0)
    q_img, feats_img = (block_img[:, :dt], block_img[:, dt:])
    q_txt, feats_txt = (block_txt[:, :dt], block_txt[:, dt:])
    e_img, inv_img = project(feats_img, proj_img)
    e_txt, inv_txt = project(feats_txt, proj_txt)
    s_img = e_img.astype(BF16)
    s_txt = e_txt.astype(BF16)
    rows, cols = (q_img.shape[0], q_txt.shape[0])

    tl = TEACHER_SCALE * jnp.dot(q_img, q_txt.T, preferred_element_type=F32)
    sl = STUDENT_SCALE * jnp.dot(s_img, s_txt.T, preferred_element_type=F32)
    rm = tl.max(1)
    cm = tl.max(0)
    er = jnp.exp(tl - rm[:, None])
    ec = jnp.exp(tl - cm[None, :])
    es = jnp.exp(sl)
    row_stats = jnp.stack([rm, er.sum(1), es.sum(1)]).reshape(3, 2, -1)
    col_stats = jnp.stack([cm, ec.sum(0), es.sum(0)])
    row_stats = jnp.where(core == 0, row_stats, row_stats[:, ::-1])
    row_all = spread(row_stats.reshape(-1, 128), TILE).reshape(-1, 3, rows)
    col_all = spread(col_stats.reshape(-1, 128), RING).reshape(-1, 3, cols)
    row_top, row_t, row_s = merge(row_all)
    col_top, col_t, col_s = merge(col_all)
    row_lse = jnp.sum(jnp.log(row_s) - row_top - jnp.log(row_t))
    col_lse = jnp.sum(jnp.log(col_s) - col_top - jnp.log(col_t))
    mine = jnp.stack([row_top, 1.0 / row_t, 1.0 / row_s]).reshape(3, 2, -1)
    mine = jnp.where(core == 0, mine, mine[:, ::-1]).reshape(3, rows)
    row_gain = jnp.exp(rm - mine[0]) * mine[1]
    col_gain = jnp.exp(cm - col_top) / col_t
    pt = er * row_gain[:, None] + ec * col_gain[None, :]
    ps = es * mine[2][:, None] + es * (1.0 / col_s)[None, :]
    total = jnp.sum(pt * (tl - sl))
    total = total + row_lse / lax.axis_size(TILE) + col_lse / lax.axis_size(RING)
    g = (0.5 * STUDENT_SCALE * (ps - pt)).astype(BF16)
    d_img = jnp.dot(g, s_txt, preferred_element_type=F32)
    d_txt = lax.dot_general(g, s_img, (((0,), (0,)), ((), ())), preferred_element_type=F32)
    du_img = tangent(d_img, e_img, inv_img).astype(BF16)
    du_txt = tangent(d_txt, e_txt, inv_txt).astype(BF16)
    rows_first = (((0,), (0,)), ((), ()))
    w_img = lax.dot_general(feats_img, du_img, rows_first, preferred_element_type=F32)
    w_txt = lax.dot_general(feats_txt, du_txt, rows_first, preferred_element_type=F32)

    width = w_img.shape[1]
    peers = lax.axis_size(PLANE)
    w_img = w_img.astype(BF16).reshape(2, peers, -1, width)
    w_txt = w_txt.astype(BF16).reshape(2, peers, -1, width)
    cut = w_img.shape[2]
    part = jnp.concatenate([w_img, w_txt], 2)
    chunk = part.shape[2]
    part = lax.all_to_all(part, "core", 0, 0, tiled=True).astype(F32).sum(0).astype(BF16)
    part = lax.all_to_all(part, PLANE, 0, 0, tiled=True).astype(F32).sum(0)
    part = lax.all_gather(with_loss(part, total), RING).astype(F32)
    chunk_sum = part[:, :chunk].sum(0)
    ring_loss = part[:, chunk, :3].sum()
    own = spread(with_loss(chunk_sum, ring_loss), PLANE)
    other = swap_cores(own)
    first = jnp.where(core == 0, own, other)
    second = jnp.where(core == 0, other, own)
    full = jnp.stack([first, second]).astype(F32)
    grad_img = full[:, :, :cut].reshape(-1, width)
    grad_txt = full[:, :, cut:chunk].reshape(-1, width)
    batch_total = image_feats.shape[0] * lax.axis_size(AXES)
    loss = full[:, :, chunk, :3].sum() / (2.0 * batch_total)
    return (loss, grad_img, grad_txt)


def solution(mesh):
    fine = Mesh(mesh.devices.reshape(SIZES), AXES)
    img = P(("zl", "core", "y", "zh", "x"), None)
    txt = P(("y", "zh", "x", "zl", "core"), None)
    return jax.shard_map(
        shards,
        mesh=fine,
        in_specs=(img, txt, img, txt, P(), P()),
        out_specs=(P(), P(), P()),
        check_vma=False,
    )
```

```python
import jax
import jax.numpy as jnp
from jax import lax
from jax.sharding import Mesh
from jax.sharding import PartitionSpec as P

EPS = 1e-06
TEACHER_SCALE = 100.0
STUDENT_SCALE = 50.0

AXES = ("zl", "core", "y", "zh", "x")
SIZES = (8, 2, 4, 2, 4)
PLANE = ("y", "x")
RING = ("zh", "zl")
TILE = ("core", "y", "x")

BF16 = jnp.bfloat16
F32 = jnp.float32


def project(feats, weight):
    u = jnp.dot(feats, weight, preferred_element_type=F32)
    inv = lax.rsqrt(jnp.sum(u * u, axis=1, keepdims=True) + EPS)
    return (u * inv, inv)


def normed(raw):
    x = raw.astype(F32)
    return (x * lax.rsqrt(jnp.sum(x * x, axis=1, keepdims=True) + EPS)).astype(BF16)


def tangent(grad_rows, embeds, inverse):
    return (grad_rows - embeds * jnp.sum(embeds * grad_rows, 1, keepdims=True)) * inverse


def spread(block, axes):
    count = lax.axis_size(axes)
    copies = jnp.broadcast_to(block[None], (count,) + block.shape)
    return lax.all_to_all(copies, axes, 0, 0, tiled=True)


def swap_cores(block):
    return lax.ppermute(block, "core", [(0, 1), (1, 0)])


def thirds(value):
    hi = value.astype(BF16)
    rest = value - hi.astype(F32)
    mid = rest.astype(BF16)
    low = (rest - mid.astype(F32)).astype(BF16)
    return jnp.stack([hi, mid, low])


def with_loss(rows, value):
    extra = jnp.zeros((8, rows.shape[1]), BF16)
    extra = extra.at[0, :3].set(thirds(value))
    return jnp.concatenate([rows.astype(BF16), extra], 0)


def merge(stats):
    top = jnp.max(stats[:, 0], 0)
    teacher = jnp.sum(stats[:, 1] * jnp.exp(stats[:, 0] - top[None]), 0)
    student = jnp.sum(stats[:, 2], 0)
    return (top, teacher, student)


def shards(image_feats, text_feats, teacher_img, teacher_txt, proj_img, proj_txt):
    core = lax.axis_index("core")
    dt = teacher_img.shape[1]
    pack_img = jnp.concatenate([normed(teacher_img), image_feats], 1)
    pack_txt = jnp.concatenate([normed(teacher_txt), text_feats], 1)
    half_img = spread(pack_img, PLANE)
    half_img = half_img.reshape(-1, pack_img.shape[1])
    block_txt = lax.all_gather(pack_txt, RING, axis=0, tiled=True)
    half_img, block_txt = lax.optimization_barrier((half_img, block_txt))
    other_img = swap_cores(half_img)
    block_img = jnp.concatenate([half_img, other_img], 0)
    q_img, feats_img = (block_img[:, :dt], block_img[:, dt:])
    q_txt, feats_txt = (block_txt[:, :dt], block_txt[:, dt:])
    e_img, inv_img = project(feats_img, proj_img)
    e_txt, inv_txt = project(feats_txt, proj_txt)
    s_img = e_img.astype(BF16)
    s_txt = e_txt.astype(BF16)
    rows, cols = (q_img.shape[0], q_txt.shape[0])

    tl = TEACHER_SCALE * jnp.dot(q_img, q_txt.T, preferred_element_type=F32)
    sl = STUDENT_SCALE * jnp.dot(s_img, s_txt.T, preferred_element_type=F32)
    rm = tl.max(1)
    cm = tl.max(0)
    er = jnp.exp(tl - rm[:, None])
    ec = jnp.exp(tl - cm[None, :])
    es = jnp.exp(sl)
    row_stats = jnp.stack([rm, er.sum(1), es.sum(1)]).reshape(3, 2, -1)
    col_stats = jnp.stack([cm, ec.sum(0), es.sum(0)])
    row_stats = jnp.where(core == 0, row_stats, row_stats[:, ::-1])
    row_all = spread(row_stats.reshape(-1, 128), TILE).reshape(-1, 3, rows)
    col_all = spread(col_stats.reshape(-1, 128), RING).reshape(-1, 3, cols)
    row_top, row_t, row_s = merge(row_all)
    col_top, col_t, col_s = merge(col_all)
    row_lse = jnp.sum(jnp.log(row_s) - row_top - jnp.log(row_t))
    col_lse = jnp.sum(jnp.log(col_s) - col_top - jnp.log(col_t))
    mine = jnp.stack([row_top, 1.0 / row_t, 1.0 / row_s]).reshape(3, 2, -1)
    mine = jnp.where(core == 0, mine, mine[:, ::-1]).reshape(3, rows)
    row_gain = jnp.exp(rm - mine[0]) * mine[1]
    col_gain = jnp.exp(cm - col_top) / col_t
    pt = er * row_gain[:, None] + ec * col_gain[None, :]
    ps = es * mine[2][:, None] + es * (1.0 / col_s)[None, :]
    total = jnp.sum(pt * (tl - sl))
    total = total + row_lse / lax.axis_size(TILE) + col_lse / lax.axis_size(RING)
    g = (0.5 * STUDENT_SCALE * (ps - pt)).astype(BF16)
    d_img = jnp.dot(g, s_txt, preferred_element_type=F32)
    d_txt = lax.dot_general(g, s_img, (((0,), (0,)), ((), ())), preferred_element_type=F32)
    du_img = tangent(d_img, e_img, inv_img).astype(BF16)
    du_txt = tangent(d_txt, e_txt, inv_txt).astype(BF16)
    rows_first = (((0,), (0,)), ((), ()))
    w_img = lax.dot_general(feats_img, du_img, rows_first, preferred_element_type=F32)
    w_txt = lax.dot_general(feats_txt, du_txt, rows_first, preferred_element_type=F32)

    width = w_img.shape[1]
    peers = lax.axis_size(PLANE)
    w_img = w_img.astype(BF16).reshape(2, peers, -1, width)
    w_txt = w_txt.astype(BF16).reshape(2, peers, -1, width)
    cut = w_img.shape[2]
    part = jnp.concatenate([w_img, w_txt], 2)
    chunk = part.shape[2]
    part = lax.all_to_all(part, "core", 0, 0, tiled=True).astype(F32).sum(0).astype(BF16)
    part = lax.all_to_all(part, PLANE, 0, 0, tiled=True).astype(F32).sum(0)
    part = lax.all_gather(with_loss(part, total), RING).astype(F32)
    chunk_sum = part[:, :chunk].sum(0)
    ring_loss = part[:, chunk, :3].sum()
    own = spread(with_loss(chunk_sum, ring_loss), PLANE)
    other = swap_cores(own)
    first = jnp.where(core == 0, own, other)
    second = jnp.where(core == 0, other, own)
    full = jnp.stack([first, second]).astype(F32)
    grad_img = full[:, :, :cut].reshape(-1, width)
    grad_txt = full[:, :, cut:chunk].reshape(-1, width)
    batch_total = image_feats.shape[0] * lax.axis_size(AXES)
    loss = full[:, :, chunk, :3].sum() / (2.0 * batch_total)
    return (loss, grad_img, grad_txt)


def solution(mesh):
    fine = Mesh(mesh.devices.reshape(SIZES), AXES)
    img = P(("zl", "core", "y", "zh", "x"), None)
    txt = P(("y", "zh", "x", "zl", "core"), None)
    return jax.shard_map(
        shards,
        mesh=fine,
        in_specs=(img, txt, img, txt, P(), P()),
        out_specs=(P(), P(), P()),
        check_vma=False,
    )
```

```python
import jax
import jax.numpy as jnp
from jax import lax
from jax.sharding import Mesh
from jax.sharding import PartitionSpec as P

EPS = 1e-06
TEACHER_SCALE = 100.0
STUDENT_SCALE = 50.0

AXES = ("zm", "zn", "core", "y", "zh", "x")
SIZES = (2, 4, 2, 4, 2, 4)
PLANE = ("y", "x")
RING = ("zh", "zm", "zn")
TILE = ("core", "y", "x")

BF16 = jnp.bfloat16
F32 = jnp.float32


def project(feats, weight):
    u = jnp.dot(feats, weight, preferred_element_type=F32)
    inv = lax.rsqrt(jnp.sum(u * u, axis=1, keepdims=True) + EPS)
    return (u * inv, inv)


def normed(raw):
    x = raw.astype(F32)
    return (x * lax.rsqrt(jnp.sum(x * x, axis=1, keepdims=True) + EPS)).astype(BF16)


def tangent(grad_rows, embeds, inverse):
    return (grad_rows - embeds * jnp.sum(embeds * grad_rows, 1, keepdims=True)) * inverse


def spread(block, axes):
    count = lax.axis_size(axes)
    copies = jnp.broadcast_to(block[None], (count,) + block.shape)
    return lax.all_to_all(copies, axes, 0, 0, tiled=True)


def swap_cores(block):
    return lax.ppermute(block, "core", [(0, 1), (1, 0)])


def thirds(value):
    hi = value.astype(BF16)
    rest = value - hi.astype(F32)
    mid = rest.astype(BF16)
    low = (rest - mid.astype(F32)).astype(BF16)
    return jnp.stack([hi, mid, low])


def with_loss(rows, value):
    extra = jnp.zeros((8, rows.shape[1]), BF16)
    extra = extra.at[0, :3].set(thirds(value))
    return jnp.concatenate([rows.astype(BF16), extra], 0)


def merge(stats):
    top = jnp.max(stats[:, 0], 0)
    teacher = jnp.sum(stats[:, 1] * jnp.exp(stats[:, 0] - top[None]), 0)
    student = jnp.sum(stats[:, 2], 0)
    return (top, teacher, student)


def shards(image_feats, text_feats, teacher_img, teacher_txt, proj_img, proj_txt):
    core = lax.axis_index("core")
    dt = teacher_img.shape[1]
    pack_img = jnp.concatenate([normed(teacher_img), image_feats], 1)
    pack_txt = jnp.concatenate([normed(teacher_txt), text_feats], 1)
    block_img = spread(pack_img, TILE).reshape(-1, pack_img.shape[1])
    block_txt = lax.all_gather(pack_txt, RING, axis=0, tiled=True)
    block_img, block_txt = lax.optimization_barrier((block_img, block_txt))
    q_img, feats_img = (block_img[:, :dt], block_img[:, dt:])
    q_txt, feats_txt = (block_txt[:, :dt], block_txt[:, dt:])
    e_img, inv_img = project(feats_img, proj_img)
    e_txt, inv_txt = project(feats_txt, proj_txt)
    s_img = e_img.astype(BF16)
    s_txt = e_txt.astype(BF16)
    rows, cols = (q_img.shape[0], q_txt.shape[0])

    tl = TEACHER_SCALE * jnp.dot(q_img, q_txt.T, preferred_element_type=F32)
    sl = STUDENT_SCALE * jnp.dot(s_img, s_txt.T, preferred_element_type=F32)
    rm = tl.max(1)
    cm = tl.max(0)
    er = jnp.exp(tl - rm[:, None])
    ec = jnp.exp(tl - cm[None, :])
    es = jnp.exp(sl)
    row_stats = jnp.stack([rm, er.sum(1), es.sum(1)]).reshape(3, 2, -1)
    col_stats = jnp.stack([cm, ec.sum(0), es.sum(0)])
    row_all = spread(row_stats.reshape(-1, 128), TILE).reshape(-1, 3, rows)
    col_all = spread(col_stats.reshape(-1, 128), RING).reshape(-1, 3, cols)
    row_top, row_t, row_s = merge(row_all)
    col_top, col_t, col_s = merge(col_all)
    row_lse = jnp.sum(jnp.log(row_s) - row_top - jnp.log(row_t))
    col_lse = jnp.sum(jnp.log(col_s) - col_top - jnp.log(col_t))
    mine = jnp.stack([row_top, 1.0 / row_t, 1.0 / row_s]).reshape(3, 2, -1)
    mine = mine.reshape(3, rows)
    row_gain = jnp.exp(rm - mine[0]) * mine[1]
    col_gain = jnp.exp(cm - col_top) / col_t
    pt = er * row_gain[:, None] + ec * col_gain[None, :]
    ps = es * mine[2][:, None] + es * (1.0 / col_s)[None, :]
    total = jnp.sum(pt * (tl - sl))
    total = total + row_lse / lax.axis_size(TILE) + col_lse / lax.axis_size(RING)
    g = (0.5 * STUDENT_SCALE * (ps - pt)).astype(BF16)
    d_img = jnp.dot(g, s_txt, preferred_element_type=F32)
    d_txt = lax.dot_general(g, s_img, (((0,), (0,)), ((), ())), preferred_element_type=F32)
    du_img = tangent(d_img, e_img, inv_img).astype(BF16)
    du_txt = tangent(d_txt, e_txt, inv_txt).astype(BF16)
    rows_first = (((0,), (0,)), ((), ()))
    w_img = lax.dot_general(feats_img, du_img, rows_first, preferred_element_type=F32)
    w_txt = lax.dot_general(feats_txt, du_txt, rows_first, preferred_element_type=F32)

    width = w_img.shape[1]
    peers = lax.axis_size(PLANE)
    w_img = w_img.astype(BF16).reshape(2, peers, -1, width)
    w_txt = w_txt.astype(BF16).reshape(2, peers, -1, width)
    cut = w_img.shape[2]
    part = jnp.concatenate([w_img, w_txt], 2)
    chunk = part.shape[2]
    part = lax.all_to_all(part, "core", 0, 0, tiled=True).astype(F32).sum(0).astype(BF16)
    part = lax.all_to_all(part, PLANE, 0, 0, tiled=True).astype(F32).sum(0)
    part = spread(with_loss(part, total), ("zn",)).astype(F32)
    mid_loss = part[:, chunk, :3].sum()
    part = spread(with_loss(part[:, :chunk].sum(0), mid_loss), ("zh", "zm")).astype(F32)
    chunk_sum = part[:, :chunk].sum(0)
    ring_loss = part[:, chunk, :3].sum()
    own = spread(with_loss(chunk_sum, ring_loss), PLANE)
    other = swap_cores(own)
    first = jnp.where(core == 0, own, other)
    second = jnp.where(core == 0, other, own)
    full = jnp.stack([first, second]).astype(F32)
    grad_img = full[:, :, :cut].reshape(-1, width)
    grad_txt = full[:, :, cut:chunk].reshape(-1, width)
    batch_total = image_feats.shape[0] * lax.axis_size(AXES)
    loss = full[:, :, chunk, :3].sum() / (2.0 * batch_total)
    return (loss, grad_img, grad_txt)


def solution(mesh):
    fine = Mesh(mesh.devices.reshape(SIZES), AXES)
    img = P(("zm", "zn", "core", "y", "zh", "x"), None)
    txt = P(("y", "zh", "x", "zm", "zn", "core"), None)
    return jax.shard_map(
        shards,
        mesh=fine,
        in_specs=(img, txt, img, txt, P(), P()),
        out_specs=(P(), P(), P()),
        check_vma=False,
    )
```

```python
import functools

import jax
import jax.numpy as jnp
from jax import lax
from jax.experimental import pallas as pl
from jax.experimental.pallas import tpu as pltpu
from jax.sharding import Mesh
from jax.sharding import PartitionSpec as P

EPS = 1e-06
TEACHER_SCALE = 100.0
STUDENT_SCALE = 50.0

AXES = ("zm", "zn", "core", "y", "zh", "x")
SIZES = (2, 4, 2, 4, 2, 4)
PLANE = ("y", "x")
NEAR = ("zn",)
FAR = ("zh", "zm")
RING = FAR + NEAR
TILE = ("core", "y", "x")

BF16 = jnp.bfloat16
F32 = jnp.float32
LANES = 128
TALL = 96
CHUNK = 160
BOX = 176

NT = (((1,), (1,)), ((), ()))
TN = (((0,), (0,)), ((), ()))
PARAMS = pltpu.CompilerParams(vmem_limit_bytes=48 * 1024 * 1024)


def call(body, outs, *args, scalars=0):
    vmem = pl.BlockSpec(memory_space=pltpu.VMEM)
    smem = pl.BlockSpec(memory_space=pltpu.SMEM)
    specs = [smem] * scalars + [vmem] * (len(args) - scalars)
    shapes = [jax.ShapeDtypeStruct(s, t) for s, t in outs]
    return pl.pallas_call(
        body,
        out_shape=shapes,
        in_specs=specs,
        out_specs=[vmem] * len(outs),
        compiler_params=PARAMS,
    )(*args)


def dot(a, b, dims=(((1,), (0,)), ((), ()))):
    return lax.dot_general(a, b, dims, preferred_element_type=F32)


def normed(raw):
    x = raw.astype(F32)
    return (x * lax.rsqrt(jnp.sum(x * x, axis=1, keepdims=True) + EPS)).astype(BF16)


def pack_body(teach_img, feats_img, teach_txt, feats_txt, out_img, out_txt):
    width = teach_img.shape[1]
    q = normed(teach_img[...])
    f = feats_img[...]
    for k in range(out_img.shape[0]):
        out_img[k, :, :width] = q
        out_img[k, :, width:] = f
    out_txt[:, :width] = normed(teach_txt[...])
    out_txt[:, width:] = feats_txt[...]


def project(feats, weight):
    u = dot(feats, weight)
    inv = lax.rsqrt(jnp.sum(u * u, axis=1, keepdims=True) + EPS)
    return (u * inv, inv)


def lse(x, axis):
    top = jnp.max(x, axis, keepdims=True)
    return top + jnp.log(jnp.sum(jnp.exp(x - top), axis, keepdims=True))


def tile_body(width, img, txt, w_img, w_txt, row_out, col_out, tl_out, sl_out, e_img, e_txt, inv_img, inv_txt):
    ei, vi = project(img[:, width:], w_img[...])
    et, vt = project(txt[:, width:], w_txt[...])
    e_img[...] = ei
    inv_img[...] = vi
    e_txt[...] = et
    inv_txt[...] = vt
    tl = TEACHER_SCALE * dot(img[:, :width], txt[:, :width], NT)
    sl = STUDENT_SCALE * dot(ei.astype(BF16), et.astype(BF16), NT)
    tl_out[...] = tl
    sl_out[...] = sl
    es = jnp.exp(sl)
    row_t = lse(tl, 1)
    row_s = jnp.log(jnp.sum(es, 1, keepdims=True))
    col_t = lse(tl, 0)
    col_s = jnp.log(jnp.sum(es, 0, keepdims=True))
    rows, cols = tl.shape
    lane = lax.broadcasted_iota(jnp.int32, (rows, LANES), 1)
    turned = jnp.where(lane == 0, row_t, row_s).T
    row_out[0] = jnp.zeros((8, LANES), F32)
    for b in range(rows // LANES):
        row_out[0, 2 * b : 2 * b + 2, :] = turned[0:2, b * LANES : (b + 1) * LANES]
    rep = row_out[0]
    for k in range(1, row_out.shape[0]):
        row_out[k] = rep
    col_out[0] = jnp.zeros((8, LANES), F32)
    for b in range(cols // LANES):
        col_out[0, b : b + 1, :] = col_t[:, b * LANES : (b + 1) * LANES]
        col_out[0, 2 + b : 3 + b, :] = col_s[:, b * LANES : (b + 1) * LANES]
    rep = col_out[0]
    for k in range(1, col_out.shape[0]):
        col_out[k] = rep


def tangent(grad_rows, embeds, inverse):
    return (grad_rows - embeds * jnp.sum(embeds * grad_rows, 1, keepdims=True)) * inverse


def grad_body(
    width, core, row_all, col_all, tl, sl, e_img, e_txt, inv_img, inv_txt, img, txt, keep, send, loss, g, wi, wt
):
    rows, cols = tl.shape
    row_parts, col_parts = (row_all.shape[0], col_all.shape[0])
    row = lse(row_all[...], 0)[0]
    col = lse(col_all[...], 0)[0]
    sub = lax.broadcasted_iota(jnp.int32, (8, LANES), 0)
    row_term = jnp.where(sub % 2 == 1, row, -row)
    col_term = jnp.where(sub < 2, -col, jnp.where(sub < 4, col, 0.0))
    total = jnp.sum(row_term, keepdims=True) / row_parts + jnp.sum(col_term, keepdims=True) / col_parts
    down = row.T
    col_t = jnp.concatenate([col[0:1], col[1:2]], 1)
    col_s = jnp.concatenate([col[2:3], col[3:4]], 1)
    acc = jnp.zeros((LANES, cols), F32)
    for b in range(rows // LANES):
        at = pl.ds(b * LANES, LANES)
        t = tl[at, :]
        s = sl[at, :]
        pt_row = jnp.exp(t - down[:, 2 * b : 2 * b + 1])
        ps_row = jnp.exp(s - down[:, 2 * b + 1 : 2 * b + 2])
        pt_col = jnp.exp(t - col_t)
        ps_col = jnp.exp(s - col_s)
        acc = acc + (pt_row + pt_col) * (t - s)
        g[at, :] = (0.5 * STUDENT_SCALE * ((ps_row - pt_row) + (ps_col - pt_col))).astype(BF16)
    total = total + jnp.sum(acc, keepdims=True)
    loss[...] = jnp.broadcast_to(total, (8, LANES))
    ei = e_img[...]
    et = e_txt[...]
    gb = g[...]
    di = dot(gb, et.astype(BF16))
    dt = dot(gb, ei.astype(BF16), TN)
    wi[...] = dot(img[:, width:], tangent(di, ei, inv_img[...]).astype(BF16), TN).astype(BF16)
    wt[...] = dot(txt[:, width:], tangent(dt, et, inv_txt[...]).astype(BF16), TN).astype(BF16)
    hi, ht = (wi.shape[0] // 2, wt.shape[0] // 2)
    me = core[0]
    for out, who in ((keep, me), (send, 1 - me)):
        a = wi[pl.ds(pl.multiple_of(who * hi, hi), hi), :]
        b = wt[pl.ds(pl.multiple_of(who * ht, ht), ht), :]
        tall, low = (TALL, CHUNK - TALL)
        for p in range(out.shape[0]):
            i, j = divmod(p, 4)
            lanes = slice(j * LANES, (j + 1) * LANES)
            out[p, :tall, :] = a[i * tall : (i + 1) * tall, lanes]
            out[p, tall:, :] = b[i * low : (i + 1) * low, lanes]


def pair_body(a, b, out):
    out[...] = (a[...].astype(F32) + b[...].astype(F32)).astype(BF16)


def thirds(value):
    hi = value.astype(BF16).astype(F32)
    mid = (value - hi).astype(BF16).astype(F32)
    low = value - hi - mid
    lane = lax.broadcasted_iota(jnp.int32, value.shape, 1)
    split = jnp.where(lane == 0, hi, jnp.where(lane == 1, mid, jnp.where(lane == 2, low, 0.0)))
    return split.astype(BF16)


def fold_body(parts, *refs):
    out = refs[-1]
    whole = jnp.sum(parts[:, :CHUNK, :].astype(F32), 0).astype(BF16)
    if len(refs) > 1:
        value = jnp.concatenate([refs[0][...]] * 2, 0)
    else:
        terms = jnp.sum(parts[:, CHUNK:, :].astype(F32), 0)
        value = jnp.broadcast_to(jnp.sum(terms, 1, keepdims=True), (BOX - CHUNK, LANES))
    split = thirds(value)
    for k in range(out.shape[0]):
        out[k, :CHUNK, :] = whole
        out[k, CHUNK:, :] = split


def output_body(scale, core, own, other, loss, grad_img, grad_txt):
    hi, ht = (grad_img.shape[0] // 2, grad_txt.shape[0] // 2)
    me = core[0]
    tall, low = (TALL, CHUNK - TALL)
    sums = []
    for box, who in ((own, me), (other, 1 - me)):
        for p in range(box.shape[0]):
            i, j = divmod(p, 4)
            lanes = slice(j * LANES, (j + 1) * LANES)
            at = pl.multiple_of(who * hi + i * tall, 8)
            grad_img[pl.ds(at, tall), lanes] = box[p, :tall, :].astype(F32)
            at = pl.multiple_of(who * ht + i * low, 8)
            grad_txt[pl.ds(at, low), lanes] = box[p, tall:CHUNK, :].astype(F32)
        terms = jnp.sum(box[:, CHUNK:, :].astype(F32), 0)
        sums.append(jnp.sum(terms, 1, keepdims=True)[:8])
    loss[...] = jnp.broadcast_to((sums[0] + sums[1]) * scale, (8, LANES))


def exchange(copies, axes):
    return lax.all_to_all(copies, axes, 0, 0, tiled=True)


def swap_cores(block):
    return lax.ppermute(block, "core", [(0, 1), (1, 0)])


def shards(image_feats, text_feats, teacher_img, teacher_txt, proj_img, proj_txt):
    core = lax.axis_index("core").reshape(1)
    n_tile, n_ring, n_plane = (lax.axis_size(a) for a in (TILE, RING, PLANE))
    n_near, n_far = (lax.axis_size(a) for a in (NEAR, FAR))
    own, width = teacher_img.shape
    wide_i = width + image_feats.shape[1]
    wide_t = width + text_feats.shape[1]
    rows, cols = (own * n_tile, own * n_ring)
    depth = proj_img.shape[1]

    pack_img, pack_txt = call(
        pack_body,
        [((n_tile, own, wide_i), BF16), ((own, wide_t), BF16)],
        teacher_img,
        image_feats,
        teacher_txt,
        text_feats,
    )
    img = exchange(pack_img, TILE).reshape(rows, wide_i)
    txt = lax.all_gather(pack_txt, RING, axis=0, tiled=True)

    row_part, col_part, *kept = call(
        functools.partial(tile_body, width),
        [
            ((n_tile, 8, LANES), F32),
            ((n_ring, 8, LANES), F32),
            ((rows, cols), F32),
            ((rows, cols), F32),
            ((rows, depth), F32),
            ((cols, depth), F32),
            ((rows, 1), F32),
            ((cols, 1), F32),
        ],
        img,
        txt,
        proj_img,
        proj_txt,
    )
    row_all = exchange(row_part, TILE)
    col_all = exchange(col_part, RING)

    box = (n_plane, CHUNK, LANES)
    vmem = pl.BlockSpec(memory_space=pltpu.VMEM)
    keep, send, total = pl.pallas_call(
        functools.partial(grad_body, width),
        out_shape=[
            jax.ShapeDtypeStruct(box, BF16),
            jax.ShapeDtypeStruct(box, BF16),
            jax.ShapeDtypeStruct((8, LANES), F32),
        ],
        in_specs=[pl.BlockSpec(memory_space=pltpu.SMEM)] + [vmem] * 10,
        out_specs=[vmem] * 3,
        scratch_shapes=[
            pltpu.VMEM((rows, cols), BF16),
            pltpu.VMEM(proj_img.shape, BF16),
            pltpu.VMEM(proj_txt.shape, BF16),
        ],
        compiler_params=PARAMS,
    )(core, row_all, col_all, *kept, img, txt)

    (part,) = call(pair_body, [(box, BF16)], keep, swap_cores(send))
    part = exchange(part, PLANE)
    (part,) = call(fold_body, [((n_near, BOX, LANES), BF16)], part, total)
    part = exchange(part, NEAR)
    (part,) = call(fold_body, [((n_far, BOX, LANES), BF16)], part)
    part = exchange(part, FAR)
    (part,) = call(fold_body, [((n_plane, BOX, LANES), BF16)], part)
    mine = exchange(part, PLANE)
    other = swap_cores(mine)
    batch_total = own * lax.axis_size(AXES)
    loss, grad_img, grad_txt = call(
        functools.partial(output_body, 1.0 / (2.0 * batch_total)),
        [((8, LANES), F32), (proj_img.shape, F32), (proj_txt.shape, F32)],
        core,
        mine,
        other,
        scalars=1,
    )
    return (loss[0, 0], grad_img, grad_txt)


def solution(mesh):
    fine = Mesh(mesh.devices.reshape(SIZES), AXES)
    img = P(("zm", "zn", "core", "y", "zh", "x"), None)
    txt = P(("y", "zh", "x", "zm", "zn", "core"), None)
    return jax.shard_map(
        shards,
        mesh=fine,
        in_specs=(img, txt, img, txt, P(), P()),
        out_specs=(P(), P(), P()),
        check_vma=False,
    )
```

```python
import functools

import jax
import jax.numpy as jnp
from jax import lax
from jax.experimental import pallas as pl
from jax.experimental.pallas import tpu as pltpu
from jax.sharding import Mesh
from jax.sharding import PartitionSpec as P

EPS = 1e-06
TEACHER_SCALE = 100.0
STUDENT_SCALE = 50.0

AXES = ("zm", "zn", "core", "y", "zh", "x")
SIZES = (2, 4, 2, 4, 2, 4)
PLANE = ("y", "x")
NEAR = ("zn",)
FAR = ("zh", "zm")
RING = FAR + NEAR
TILE = ("core", "y", "x")

BF16 = jnp.bfloat16
F32 = jnp.float32
LANES = 128
TALL = 96
CHUNK = 160
BOX = 176

NT = (((1,), (1,)), ((), ()))
TN = (((0,), (0,)), ((), ()))


def room(mib):
    return pltpu.CompilerParams(vmem_limit_bytes=mib * 1024 * 1024)


def call(body, mib, outs, *args, scalars=0):
    vmem = pl.BlockSpec(memory_space=pltpu.VMEM)
    smem = pl.BlockSpec(memory_space=pltpu.SMEM)
    specs = [smem] * scalars + [vmem] * (len(args) - scalars)
    shapes = [jax.ShapeDtypeStruct(s, t) for s, t in outs]
    return pl.pallas_call(
        body,
        out_shape=shapes,
        in_specs=specs,
        out_specs=[vmem] * len(outs),
        compiler_params=room(mib),
    )(*args)


def fetch(sources, held, sems):
    copies = [pltpu.make_async_copy(a, b, sems.at[k]) for k, (a, b) in enumerate(zip(sources, held))]
    for c in copies:
        c.start()
    return copies


def pinned(array):
    return pltpu.with_memory_space_constraint(array, pltpu.HBM)


HBM = pl.BlockSpec(memory_space=pltpu.HBM)
VMEM = pl.BlockSpec(memory_space=pltpu.VMEM)
SMEM = pl.BlockSpec(memory_space=pltpu.SMEM)


def dot(a, b, dims=(((1,), (0,)), ((), ()))):
    return lax.dot_general(a, b, dims, preferred_element_type=F32)


def normed(raw):
    x = raw.astype(F32)
    return (x * lax.rsqrt(jnp.sum(x * x, axis=1, keepdims=True) + EPS)).astype(BF16)


def pack_body(*refs):
    ins, (out_img, out_txt), held = refs[:4], refs[4:6], refs[6:10]
    row_img, row_txt, in_sems, out_sems = refs[10:]
    copies = fetch(ins, held, in_sems)
    teach_img, feats_img, teach_txt, feats_txt = held
    width = teach_img.shape[1]
    copies[0].wait()
    copies[1].wait()
    row_img[:, :width] = normed(teach_img[...])
    row_img[:, width:] = feats_img[...]
    peers = out_img.shape[0]
    sent = fetch([row_img] * peers, [out_img.at[k] for k in range(peers)], out_sems)
    copies[2].wait()
    copies[3].wait()
    row_txt[:, :width] = normed(teach_txt[...])
    row_txt[:, width:] = feats_txt[...]
    last = pltpu.make_async_copy(row_txt, out_txt, in_sems.at[0])
    last.start()
    for c in sent:
        c.wait()
    last.wait()


def scale_of(u):
    return lax.rsqrt(jnp.sum(u * u, axis=1, keepdims=True) + EPS)


def lse(x, axis):
    top = jnp.max(x, axis, keepdims=True)
    return top + jnp.log(jnp.sum(jnp.exp(x - top), axis, keepdims=True))


def tile_body(width, img, txt, *refs):
    ins, (row_out, col_out), outs = refs[:2], refs[2:4], refs[4:10]
    w_img, w_txt = refs[10:12]
    made = refs[12:16]
    in_sems, out_sems = refs[16:]
    copies = fetch(ins, (w_img, w_txt), in_sems)
    tl_own, sl_own, u_img, u_txt = made
    sources = list(made) + [img.at[:, width:], txt.at[:, width:]]
    back = [pltpu.make_async_copy(sources[k], outs[k], out_sems.at[k]) for k in range(6)]
    back[4].start()
    back[5].start()
    tl_own[...] = TEACHER_SCALE * dot(img[:, :width], txt[:, :width], NT)
    back[0].start()
    copies[0].wait()
    u_img[...] = dot(img[:, width:], w_img[...])
    back[2].start()
    copies[1].wait()
    u_txt[...] = dot(txt[:, width:], w_txt[...])
    back[3].start()
    ui = u_img[...]
    ut = u_txt[...]
    ei = (ui * scale_of(ui)).astype(BF16)
    et = (ut * scale_of(ut)).astype(BF16)
    sl_own[...] = STUDENT_SCALE * dot(ei, et, NT)
    back[1].start()
    tl = tl_own[...]
    sl = sl_own[...]
    es = jnp.exp(sl)
    rows, cols = tl.shape
    row_t = lse(tl, 1)
    row_s = jnp.log(jnp.sum(es, 1, keepdims=True))
    lane = lax.broadcasted_iota(jnp.int32, (rows, LANES), 1)
    turned = jnp.where(lane == 0, row_t, row_s).T
    row_out[0] = jnp.zeros((8, LANES), F32)
    for b in range(rows // LANES):
        row_out[0, 2 * b : 2 * b + 2, :] = turned[0:2, b * LANES : (b + 1) * LANES]
    rep = row_out[0]
    for k in range(1, row_out.shape[0]):
        row_out[k] = rep
    col_t = lse(tl, 0)
    col_s = jnp.log(jnp.sum(es, 0, keepdims=True))
    col_out[0] = jnp.zeros((8, LANES), F32)
    for b in range(cols // LANES):
        col_out[0, b : b + 1, :] = col_t[:, b * LANES : (b + 1) * LANES]
        col_out[0, 2 + b : 3 + b, :] = col_s[:, b * LANES : (b + 1) * LANES]
    rep = col_out[0]
    for k in range(1, col_out.shape[0]):
        col_out[k] = rep
    for c in back:
        c.wait()


def tangent(grad_rows, embeds, inverse):
    return (grad_rows - embeds * jnp.sum(embeds * grad_rows, 1, keepdims=True)) * inverse


def grad_body(core, row_all, col_all, *refs):
    ins, (keep, send, loss), held, (g, wi, wt, sems) = refs[:6], refs[6:9], refs[9:15], refs[15:]
    copies = fetch(ins, held, sems)
    tl, sl, u_img, u_txt, feats_img, feats_txt = held
    rows, cols = tl.shape
    row_parts, col_parts = (row_all.shape[0], col_all.shape[0])
    row = lse(row_all[...], 0)[0]
    col = lse(col_all[...], 0)[0]
    sub = lax.broadcasted_iota(jnp.int32, (8, LANES), 0)
    row_term = jnp.where(sub % 2 == 1, row, -row)
    col_term = jnp.where(sub < 2, -col, jnp.where(sub < 4, col, 0.0))
    total = jnp.sum(row_term, keepdims=True) / row_parts + jnp.sum(col_term, keepdims=True) / col_parts
    down = row.T
    col_t = jnp.concatenate([col[0:1], col[1:2]], 1)
    col_s = jnp.concatenate([col[2:3], col[3:4]], 1)
    acc = jnp.zeros((LANES, cols), F32)
    copies[0].wait()
    copies[1].wait()
    for b in range(rows // LANES):
        at = pl.ds(b * LANES, LANES)
        t = tl[at, :]
        s = sl[at, :]
        pt_row = jnp.exp(t - down[:, 2 * b : 2 * b + 1])
        ps_row = jnp.exp(s - down[:, 2 * b + 1 : 2 * b + 2])
        pt_col = jnp.exp(t - col_t)
        ps_col = jnp.exp(s - col_s)
        acc = acc + (pt_row + pt_col) * (t - s)
        g[at, :] = (0.5 * STUDENT_SCALE * ((ps_row - pt_row) + (ps_col - pt_col))).astype(BF16)
    total = total + jnp.sum(acc, keepdims=True)
    loss[...] = jnp.broadcast_to(total, (8, LANES))
    for c in copies[2:]:
        c.wait()
    ui = u_img[...]
    ut = u_txt[...]
    inv_img = scale_of(ui)
    inv_txt = scale_of(ut)
    ei = ui * inv_img
    et = ut * inv_txt
    gb = g[...]
    di = dot(gb, et.astype(BF16))
    dt = dot(gb, ei.astype(BF16), TN)
    wi[...] = dot(feats_img[...], tangent(di, ei, inv_img).astype(BF16), TN).astype(BF16)
    wt[...] = dot(feats_txt[...], tangent(dt, et, inv_txt).astype(BF16), TN).astype(BF16)
    hi, ht = (wi.shape[0] // 2, wt.shape[0] // 2)
    me = core[0]
    for out, who in ((keep, me), (send, 1 - me)):
        a = wi[pl.ds(pl.multiple_of(who * hi, hi), hi), :]
        b = wt[pl.ds(pl.multiple_of(who * ht, ht), ht), :]
        tall, low = (TALL, CHUNK - TALL)
        for p in range(out.shape[0]):
            i, j = divmod(p, 4)
            lanes = slice(j * LANES, (j + 1) * LANES)
            out[p, :tall, :] = a[i * tall : (i + 1) * tall, lanes]
            out[p, tall:, :] = b[i * low : (i + 1) * low, lanes]


def pair_body(a, b, out):
    out[...] = (a[...].astype(F32) + b[...].astype(F32)).astype(BF16)


def thirds(value):
    hi = value.astype(BF16).astype(F32)
    mid = (value - hi).astype(BF16).astype(F32)
    low = value - hi - mid
    lane = lax.broadcasted_iota(jnp.int32, value.shape, 1)
    split = jnp.where(lane == 0, hi, jnp.where(lane == 1, mid, jnp.where(lane == 2, low, 0.0)))
    return split.astype(BF16)


def fold_body(parts, *refs):
    out = refs[-1]
    whole = jnp.sum(parts[:, :CHUNK, :].astype(F32), 0).astype(BF16)
    if len(refs) > 1:
        value = jnp.concatenate([refs[0][...]] * 2, 0)
    else:
        terms = jnp.sum(parts[:, CHUNK:, :].astype(F32), 0)
        value = jnp.broadcast_to(jnp.sum(terms, 1, keepdims=True), (BOX - CHUNK, LANES))
    split = thirds(value)
    for k in range(out.shape[0]):
        out[k, :CHUNK, :] = whole
        out[k, CHUNK:, :] = split


def output_body(scale, core, own, other, loss, grad_img, grad_txt):
    hi, ht = (grad_img.shape[0] // 2, grad_txt.shape[0] // 2)
    me = core[0]
    tall, low = (TALL, CHUNK - TALL)
    sums = []
    for box, who in ((own, me), (other, 1 - me)):
        for p in range(box.shape[0]):
            i, j = divmod(p, 4)
            lanes = slice(j * LANES, (j + 1) * LANES)
            at = pl.multiple_of(who * hi + i * tall, 8)
            grad_img[pl.ds(at, tall), lanes] = box[p, :tall, :].astype(F32)
            at = pl.multiple_of(who * ht + i * low, 8)
            grad_txt[pl.ds(at, low), lanes] = box[p, tall:CHUNK, :].astype(F32)
        terms = jnp.sum(box[:, CHUNK:, :].astype(F32), 0)
        sums.append(jnp.sum(terms[:1], keepdims=True))
    loss[...] = (sums[0] + sums[1]) * scale


def exchange(copies, axes):
    return lax.all_to_all(copies, axes, 0, 0, tiled=True)


def swap_cores(block):
    return lax.ppermute(block, "core", [(0, 1), (1, 0)])


def shards(image_feats, text_feats, teacher_img, teacher_txt, proj_img, proj_txt):
    core = lax.axis_index("core").reshape(1)
    n_tile, n_ring, n_plane = (lax.axis_size(a) for a in (TILE, RING, PLANE))
    n_near, n_far = (lax.axis_size(a) for a in (NEAR, FAR))
    own, width = teacher_img.shape
    wide_i = width + image_feats.shape[1]
    wide_t = width + text_feats.shape[1]
    rows, cols = (own * n_tile, own * n_ring)
    depth = proj_img.shape[1]

    raw = (teacher_img, image_feats, teacher_txt, text_feats)
    pack_img, pack_txt = pl.pallas_call(
        pack_body,
        out_shape=[pltpu.HBM((n_tile, own, wide_i), BF16), pltpu.HBM((own, wide_t), BF16)],
        in_specs=[HBM] * 4,
        out_specs=[HBM] * 2,
        scratch_shapes=[pltpu.VMEM(a.shape, a.dtype) for a in raw]
        + [
            pltpu.VMEM((own, wide_i), BF16),
            pltpu.VMEM((own, wide_t), BF16),
            pltpu.SemaphoreType.DMA((4,)),
            pltpu.SemaphoreType.DMA((n_tile,)),
        ],
        compiler_params=room(8),
    )(*[pinned(a) for a in raw])
    img = exchange(pack_img, TILE).reshape(rows, wide_i)
    txt = lax.all_gather(pack_txt, RING, axis=0, tiled=True)

    blocks = [(rows, cols), (rows, cols), (rows, depth), (cols, depth)]
    feats = [(rows, proj_img.shape[0]), (cols, proj_txt.shape[0])]
    row_part, col_part, *kept = pl.pallas_call(
        functools.partial(tile_body, width),
        out_shape=[jax.ShapeDtypeStruct((n, 8, LANES), F32) for n in (n_tile, n_ring)]
        + [pltpu.HBM(b, F32) for b in blocks]
        + [pltpu.HBM(b, BF16) for b in feats],
        in_specs=[VMEM] * 2 + [HBM] * 2,
        out_specs=[VMEM] * 2 + [HBM] * 6,
        scratch_shapes=[pltpu.VMEM(a.shape, BF16) for a in (proj_img, proj_txt)]
        + [pltpu.VMEM(b, F32) for b in blocks]
        + [pltpu.SemaphoreType.DMA((n,)) for n in (2, 6)],
        compiler_params=room(24),
    )(img, txt, pinned(proj_img), pinned(proj_txt))
    row_all = exchange(row_part, TILE)
    col_all = exchange(col_part, RING)

    box = (n_plane, CHUNK, LANES)
    keep, send, total = pl.pallas_call(
        grad_body,
        out_shape=[
            jax.ShapeDtypeStruct(box, BF16),
            jax.ShapeDtypeStruct(box, BF16),
            jax.ShapeDtypeStruct((8, LANES), F32),
        ],
        in_specs=[SMEM, VMEM, VMEM] + [HBM] * 6,
        out_specs=[VMEM] * 3,
        scratch_shapes=[pltpu.VMEM(b, F32) for b in blocks]
        + [
            pltpu.VMEM(feats[0], BF16),
            pltpu.VMEM(feats[1], BF16),
            pltpu.VMEM((rows, cols), BF16),
            pltpu.VMEM(proj_img.shape, BF16),
            pltpu.VMEM(proj_txt.shape, BF16),
            pltpu.SemaphoreType.DMA((6,)),
        ],
        compiler_params=room(24),
    )(core, row_all, col_all, *[pinned(k) for k in kept])

    (part,) = call(pair_body, 8, [(box, BF16)], keep, swap_cores(send))
    part = exchange(part, PLANE)
    (part,) = call(fold_body, 8, [((n_near, BOX, LANES), BF16)], part, total)
    part = exchange(part, NEAR)
    (part,) = call(fold_body, 8, [((n_far, BOX, LANES), BF16)], part)
    part = exchange(part, FAR)
    (part,) = call(fold_body, 8, [((n_plane, BOX, LANES), BF16)], part)
    mine = exchange(part, PLANE)
    other = swap_cores(mine)
    batch_total = own * lax.axis_size(AXES)
    loss, grad_img, grad_txt = call(
        functools.partial(output_body, 1.0 / (2.0 * batch_total)),
        10,
        [((1, 1), F32), (proj_img.shape, F32), (proj_txt.shape, F32)],
        core,
        mine,
        other,
        scalars=1,
    )
    return (loss.reshape(()), grad_img, grad_txt)


def solution(mesh):
    fine = Mesh(mesh.devices.reshape(SIZES), AXES)
    img = P(("zm", "zn", "core", "y", "zh", "x"), None)
    txt = P(("y", "zh", "x", "zm", "zn", "core"), None)
    return jax.shard_map(
        shards,
        mesh=fine,
        in_specs=(img, txt, img, txt, P(), P()),
        out_specs=(P(), P(), P()),
        check_vma=False,
    )
```

```python
import functools

import jax
import jax.numpy as jnp
from jax import lax
from jax.experimental import pallas as pl
from jax.experimental.pallas import tpu as pltpu
from jax.sharding import Mesh
from jax.sharding import PartitionSpec as P

EPS = 1e-06
TEACHER_SCALE = 100.0
STUDENT_SCALE = 50.0

AXES = ("zm", "zn", "core", "y", "zh", "x")
SIZES = (2, 4, 2, 4, 2, 4)
PLANE = ("y", "x")
NEAR = ("zn",)
FAR = ("zh", "zm")
RING = FAR + NEAR
TILE = ("core", "y", "x")

BF16 = jnp.bfloat16
F32 = jnp.float32
LANES = 128
TALL = 96
CHUNK = 160
BOX = 176

NT = (((1,), (1,)), ((), ()))
TN = (((0,), (0,)), ((), ()))


def room(mib):
    return pltpu.CompilerParams(vmem_limit_bytes=mib * 1024 * 1024)


def call(body, mib, outs, *args, scalars=0):
    vmem = pl.BlockSpec(memory_space=pltpu.VMEM)
    smem = pl.BlockSpec(memory_space=pltpu.SMEM)
    specs = [smem] * scalars + [vmem] * (len(args) - scalars)
    shapes = [jax.ShapeDtypeStruct(s, t) for s, t in outs]
    return pl.pallas_call(
        body,
        out_shape=shapes,
        in_specs=specs,
        out_specs=[vmem] * len(outs),
        compiler_params=room(mib),
    )(*args)


def fetch(sources, held, sems):
    copies = [pltpu.make_async_copy(a, b, sems.at[k]) for k, (a, b) in enumerate(zip(sources, held))]
    for c in copies:
        c.start()
    return copies


def pinned(array):
    return pltpu.with_memory_space_constraint(array, pltpu.HBM)


HBM = pl.BlockSpec(memory_space=pltpu.HBM)
VMEM = pl.BlockSpec(memory_space=pltpu.VMEM)
SMEM = pl.BlockSpec(memory_space=pltpu.SMEM)


def dot(a, b, dims=(((1,), (0,)), ((), ()))):
    return lax.dot_general(a, b, dims, preferred_element_type=F32)


def normed(raw):
    x = raw.astype(F32)
    return (x * lax.rsqrt(jnp.sum(x * x, axis=1, keepdims=True) + EPS)).astype(BF16)


def pack_body(*refs):
    ins, (out_img, out_txt), held = refs[:4], refs[4:6], refs[6:10]
    row_img, row_txt, in_sems, out_sems = refs[10:]
    copies = fetch(ins, held, in_sems)
    teach_img, feats_img, teach_txt, feats_txt = held
    width = teach_img.shape[1]
    copies[0].wait()
    copies[1].wait()
    row_img[:, :width] = normed(teach_img[...])
    row_img[:, width:] = feats_img[...]
    peers = out_img.shape[0]
    sent = fetch([row_img] * peers, [out_img.at[k] for k in range(peers)], out_sems)
    copies[2].wait()
    copies[3].wait()
    row_txt[:, :width] = normed(teach_txt[...])
    row_txt[:, width:] = feats_txt[...]
    last = pltpu.make_async_copy(row_txt, out_txt, in_sems.at[0])
    last.start()
    for c in sent:
        c.wait()
    last.wait()


def scale_of(u):
    return lax.rsqrt(jnp.sum(u * u, axis=1, keepdims=True) + EPS)


def lse(x, axis):
    top = jnp.max(x, axis, keepdims=True)
    return top + jnp.log(jnp.sum(jnp.exp(x - top), axis, keepdims=True))


def tile_body(width, img, txt, w_img, w_txt_in, *refs):
    (row_out, col_out), outs, w_txt, made = refs[:2], refs[2:8], refs[8], refs[9:13]
    in_sems, out_sems = refs[13:]
    copies = fetch([w_txt_in], [w_txt], in_sems)
    tl_own, sl_own, u_img, u_txt = made
    sources = list(made) + [img.at[:, width:], txt.at[:, width:]]
    back = [pltpu.make_async_copy(sources[k], outs[k], out_sems.at[k]) for k in range(6)]
    back[4].start()
    back[5].start()
    tl_own[...] = TEACHER_SCALE * dot(img[:, :width], txt[:, :width], NT)
    back[0].start()
    u_img[...] = dot(img[:, width:], w_img[...])
    back[2].start()
    copies[0].wait()
    u_txt[...] = dot(txt[:, width:], w_txt[...])
    back[3].start()
    ui = u_img[...]
    ut = u_txt[...]
    ei = (ui * scale_of(ui)).astype(BF16)
    et = (ut * scale_of(ut)).astype(BF16)
    sl_own[...] = STUDENT_SCALE * dot(ei, et, NT)
    back[1].start()
    tl = tl_own[...]
    sl = sl_own[...]
    es = jnp.exp(sl)
    rows, cols = tl.shape
    row_t = lse(tl, 1)
    row_s = jnp.log(jnp.sum(es, 1, keepdims=True))
    lane = lax.broadcasted_iota(jnp.int32, (rows, LANES), 1)
    turned = jnp.where(lane == 0, row_t, row_s).T
    row_out[0] = jnp.zeros((8, LANES), F32)
    for b in range(rows // LANES):
        row_out[0, 2 * b : 2 * b + 2, :] = turned[0:2, b * LANES : (b + 1) * LANES]
    rep = row_out[0]
    for k in range(1, row_out.shape[0]):
        row_out[k] = rep
    col_t = lse(tl, 0)
    col_s = jnp.log(jnp.sum(es, 0, keepdims=True))
    col_out[0] = jnp.zeros((8, LANES), F32)
    for b in range(cols // LANES):
        col_out[0, b : b + 1, :] = col_t[:, b * LANES : (b + 1) * LANES]
        col_out[0, 2 + b : 3 + b, :] = col_s[:, b * LANES : (b + 1) * LANES]
    rep = col_out[0]
    for k in range(1, col_out.shape[0]):
        col_out[k] = rep
    for c in back:
        c.wait()


def tangent(grad_rows, embeds, inverse):
    return (grad_rows - embeds * jnp.sum(embeds * grad_rows, 1, keepdims=True)) * inverse


def grad_body(core, row_all, col_all, *refs):
    ins, (keep, send, loss), held, (g, wi, wt, sems) = refs[:6], refs[6:9], refs[9:15], refs[15:]
    copies = fetch(ins, held, sems)
    tl, sl, u_img, u_txt, feats_img, feats_txt = held
    rows, cols = tl.shape
    row_parts, col_parts = (row_all.shape[0], col_all.shape[0])
    row = lse(row_all[...], 0)[0]
    col = lse(col_all[...], 0)[0]
    sub = lax.broadcasted_iota(jnp.int32, (8, LANES), 0)
    row_term = jnp.where(sub % 2 == 1, row, -row)
    col_term = jnp.where(sub < 2, -col, jnp.where(sub < 4, col, 0.0))
    total = jnp.sum(row_term, keepdims=True) / row_parts + jnp.sum(col_term, keepdims=True) / col_parts
    down = row.T
    col_t = jnp.concatenate([col[0:1], col[1:2]], 1)
    col_s = jnp.concatenate([col[2:3], col[3:4]], 1)
    acc = jnp.zeros((LANES, cols), F32)
    copies[0].wait()
    copies[1].wait()
    for b in range(rows // LANES):
        at = pl.ds(b * LANES, LANES)
        t = tl[at, :]
        s = sl[at, :]
        pt_row = jnp.exp(t - down[:, 2 * b : 2 * b + 1])
        ps_row = jnp.exp(s - down[:, 2 * b + 1 : 2 * b + 2])
        pt_col = jnp.exp(t - col_t)
        ps_col = jnp.exp(s - col_s)
        acc = acc + (pt_row + pt_col) * (t - s)
        g[at, :] = (0.5 * STUDENT_SCALE * ((ps_row - pt_row) + (ps_col - pt_col))).astype(BF16)
    total = total + jnp.sum(acc, keepdims=True)
    loss[...] = jnp.broadcast_to(total, (8, LANES))
    for c in copies[2:]:
        c.wait()
    ui = u_img[...]
    ut = u_txt[...]
    inv_img = scale_of(ui)
    inv_txt = scale_of(ut)
    ei = ui * inv_img
    et = ut * inv_txt
    gb = g[...]
    di = dot(gb, et.astype(BF16))
    dt = dot(gb, ei.astype(BF16), TN)
    wi[...] = dot(feats_img[...], tangent(di, ei, inv_img).astype(BF16), TN).astype(BF16)
    wt[...] = dot(feats_txt[...], tangent(dt, et, inv_txt).astype(BF16), TN).astype(BF16)
    hi, ht = (wi.shape[0] // 2, wt.shape[0] // 2)
    me = core[0]
    for out, who in ((keep, me), (send, 1 - me)):
        a = wi[pl.ds(pl.multiple_of(who * hi, hi), hi), :]
        b = wt[pl.ds(pl.multiple_of(who * ht, ht), ht), :]
        tall, low = (TALL, CHUNK - TALL)
        for p in range(out.shape[0]):
            i, j = divmod(p, 4)
            lanes = slice(j * LANES, (j + 1) * LANES)
            out[p, :tall, :] = a[i * tall : (i + 1) * tall, lanes]
            out[p, tall:, :] = b[i * low : (i + 1) * low, lanes]


def pair_body(a, b, out):
    out[...] = (a[...].astype(F32) + b[...].astype(F32)).astype(BF16)


def thirds(value):
    hi = value.astype(BF16).astype(F32)
    mid = (value - hi).astype(BF16).astype(F32)
    low = value - hi - mid
    lane = lax.broadcasted_iota(jnp.int32, value.shape, 1)
    split = jnp.where(lane == 0, hi, jnp.where(lane == 1, mid, jnp.where(lane == 2, low, 0.0)))
    return split.astype(BF16)


def fold_body(parts, *refs):
    out = refs[-1]
    whole = jnp.sum(parts[:, :CHUNK, :].astype(F32), 0).astype(BF16)
    if len(refs) > 1:
        value = jnp.concatenate([refs[0][...]] * 2, 0)
    else:
        terms = jnp.sum(parts[:, CHUNK:, :].astype(F32), 0)
        value = jnp.broadcast_to(jnp.sum(terms, 1, keepdims=True), (BOX - CHUNK, LANES))
    split = thirds(value)
    for k in range(out.shape[0]):
        out[k, :CHUNK, :] = whole
        out[k, CHUNK:, :] = split


def output_body(scale, core, own, other, loss, grad_img, grad_txt):
    hi, ht = (grad_img.shape[0] // 2, grad_txt.shape[0] // 2)
    me = core[0]
    tall, low = (TALL, CHUNK - TALL)
    sums = []
    for box, who in ((own, me), (other, 1 - me)):
        for p in range(box.shape[0]):
            i, j = divmod(p, 4)
            lanes = slice(j * LANES, (j + 1) * LANES)
            at = pl.multiple_of(who * hi + i * tall, 8)
            grad_img[pl.ds(at, tall), lanes] = box[p, :tall, :].astype(F32)
            at = pl.multiple_of(who * ht + i * low, 8)
            grad_txt[pl.ds(at, low), lanes] = box[p, tall:CHUNK, :].astype(F32)
        terms = jnp.sum(box[:, CHUNK:, :].astype(F32), 0)
        sums.append(jnp.sum(terms[:1], keepdims=True))
    loss[...] = (sums[0] + sums[1]) * scale


def exchange(copies, axes):
    return lax.all_to_all(copies, axes, 0, 0, tiled=True)


def swap_cores(block):
    return lax.ppermute(block, "core", [(0, 1), (1, 0)])


def shards(image_feats, text_feats, teacher_img, teacher_txt, proj_img, proj_txt):
    core = lax.axis_index("core").reshape(1)
    n_tile, n_ring, n_plane = (lax.axis_size(a) for a in (TILE, RING, PLANE))
    n_near, n_far = (lax.axis_size(a) for a in (NEAR, FAR))
    own, width = teacher_img.shape
    wide_i = width + image_feats.shape[1]
    wide_t = width + text_feats.shape[1]
    rows, cols = (own * n_tile, own * n_ring)
    depth = proj_img.shape[1]

    raw = (teacher_img, image_feats, teacher_txt, text_feats)
    pack_img, pack_txt = pl.pallas_call(
        pack_body,
        out_shape=[pltpu.HBM((n_tile, own, wide_i), BF16), pltpu.HBM((own, wide_t), BF16)],
        in_specs=[HBM] * 4,
        out_specs=[HBM] * 2,
        scratch_shapes=[pltpu.VMEM(a.shape, a.dtype) for a in raw]
        + [
            pltpu.VMEM((own, wide_i), BF16),
            pltpu.VMEM((own, wide_t), BF16),
            pltpu.SemaphoreType.DMA((4,)),
            pltpu.SemaphoreType.DMA((n_tile,)),
        ],
        compiler_params=room(8),
    )(*[pinned(a) for a in raw])
    pack_img, core = lax.optimization_barrier((pack_img, core))
    img = exchange(pack_img, TILE).reshape(rows, wide_i)
    txt = lax.all_gather(pack_txt, RING, axis=0, tiled=True)

    blocks = [(rows, cols), (rows, cols), (rows, depth), (cols, depth)]
    feats = [(rows, proj_img.shape[0]), (cols, proj_txt.shape[0])]
    row_part, col_part, *kept = pl.pallas_call(
        functools.partial(tile_body, width),
        out_shape=[jax.ShapeDtypeStruct((n, 8, LANES), F32) for n in (n_tile, n_ring)]
        + [pltpu.HBM(b, F32) for b in blocks]
        + [pltpu.HBM(b, BF16) for b in feats],
        in_specs=[VMEM] * 3 + [HBM],
        out_specs=[VMEM] * 2 + [HBM] * 6,
        scratch_shapes=[pltpu.VMEM(proj_txt.shape, BF16)]
        + [pltpu.VMEM(b, F32) for b in blocks]
        + [pltpu.SemaphoreType.DMA((n,)) for n in (1, 6)],
        compiler_params=room(24),
    )(img, txt, proj_img, pinned(proj_txt))
    row_all = exchange(row_part, TILE)
    col_part, row_all = lax.optimization_barrier((col_part, row_all))
    col_all = exchange(col_part, RING)

    box = (n_plane, CHUNK, LANES)
    keep, send, total = pl.pallas_call(
        grad_body,
        out_shape=[
            jax.ShapeDtypeStruct(box, BF16),
            jax.ShapeDtypeStruct(box, BF16),
            jax.ShapeDtypeStruct((8, LANES), F32),
        ],
        in_specs=[SMEM, VMEM, VMEM] + [HBM] * 6,
        out_specs=[VMEM] * 3,
        scratch_shapes=[pltpu.VMEM(b, F32) for b in blocks]
        + [
            pltpu.VMEM(feats[0], BF16),
            pltpu.VMEM(feats[1], BF16),
            pltpu.VMEM((rows, cols), BF16),
            pltpu.VMEM(proj_img.shape, BF16),
            pltpu.VMEM(proj_txt.shape, BF16),
            pltpu.SemaphoreType.DMA((6,)),
        ],
        compiler_params=room(24),
    )(core, row_all, col_all, *[pinned(k) for k in kept])

    (part,) = call(pair_body, 8, [(box, BF16)], keep, swap_cores(send))
    part = exchange(part, PLANE)
    (part,) = call(fold_body, 8, [((n_near, BOX, LANES), BF16)], part, total)
    part = exchange(part, NEAR)
    (part,) = call(fold_body, 8, [((1, BOX, LANES), BF16)], part)
    part = lax.all_gather(part, FAR, axis=0, tiled=True)
    (part,) = call(fold_body, 8, [((n_plane, BOX, LANES), BF16)], part)
    mine = exchange(part, PLANE)
    other = swap_cores(mine)
    batch_total = own * lax.axis_size(AXES)
    loss, grad_img, grad_txt = call(
        functools.partial(output_body, 1.0 / (2.0 * batch_total)),
        10,
        [((1, 1), F32), (proj_img.shape, F32), (proj_txt.shape, F32)],
        core,
        mine,
        other,
        scalars=1,
    )
    return (loss.reshape(()), grad_img, grad_txt)


def solution(mesh):
    fine = Mesh(mesh.devices.reshape(SIZES), AXES)
    img = P(("zm", "zn", "core", "y", "zh", "x"), None)
    txt = P(("y", "zh", "x", "zm", "zn", "core"), None)
    return jax.shard_map(
        shards,
        mesh=fine,
        in_specs=(img, txt, img, txt, P(), P()),
        out_specs=(P(), P(), P()),
        check_vma=False,
    )
```

```python
import functools

import jax
import jax.numpy as jnp
from jax import lax
from jax.experimental import pallas as pl
from jax.experimental.pallas import tpu as pltpu
from jax.sharding import Mesh
from jax.sharding import PartitionSpec as P

EPS = 1e-06
TEACHER_SCALE = 100.0
STUDENT_SCALE = 50.0

AXES = ("zm", "zn", "core", "y", "zh", "x")
SIZES = (2, 4, 2, 4, 2, 4)
PLANE = ("y", "x")
NEAR = ("zn",)
FAR = ("zh", "zm")
RING = FAR + NEAR
TILE = ("core", "y", "x")

BF16 = jnp.bfloat16
F32 = jnp.float32
LANES = 128
TALL = 96
CHUNK = 160
BOX = 176

NT = (((1,), (1,)), ((), ()))
TN = (((0,), (0,)), ((), ()))


def room(mib):
    return pltpu.CompilerParams(vmem_limit_bytes=mib * 1024 * 1024)


def call(body, mib, outs, *args, scalars=0):
    vmem = pl.BlockSpec(memory_space=pltpu.VMEM)
    smem = pl.BlockSpec(memory_space=pltpu.SMEM)
    specs = [smem] * scalars + [vmem] * (len(args) - scalars)
    shapes = [jax.ShapeDtypeStruct(s, t) for s, t in outs]
    return pl.pallas_call(
        body,
        out_shape=shapes,
        in_specs=specs,
        out_specs=[vmem] * len(outs),
        compiler_params=room(mib),
    )(*args)


def fetch(sources, held, sems):
    copies = [pltpu.make_async_copy(a, b, sems.at[k]) for k, (a, b) in enumerate(zip(sources, held))]
    for c in copies:
        c.start()
    return copies


def pinned(array):
    return pltpu.with_memory_space_constraint(array, pltpu.HBM)


HBM = pl.BlockSpec(memory_space=pltpu.HBM)
VMEM = pl.BlockSpec(memory_space=pltpu.VMEM)
SMEM = pl.BlockSpec(memory_space=pltpu.SMEM)


def dot(a, b, dims=(((1,), (0,)), ((), ()))):
    return lax.dot_general(a, b, dims, preferred_element_type=F32)


def normed(raw):
    x = raw.astype(F32)
    return (x * lax.rsqrt(jnp.sum(x * x, axis=1, keepdims=True) + EPS)).astype(BF16)


def pack_body(*refs):
    ins, (out_img, out_txt), held = refs[:4], refs[4:6], refs[6:10]
    row_img, row_txt, in_sems, out_sems = refs[10:]
    copies = fetch(ins, held, in_sems)
    teach_img, feats_img, teach_txt, feats_txt = held
    width = teach_img.shape[1]
    copies[0].wait()
    copies[1].wait()
    row_img[:, :width] = normed(teach_img[...])
    row_img[:, width:] = feats_img[...]
    peers = out_img.shape[0]
    sent = fetch([row_img] * peers, [out_img.at[k] for k in range(peers)], out_sems)
    copies[2].wait()
    copies[3].wait()
    row_txt[:, :width] = normed(teach_txt[...])
    row_txt[:, width:] = feats_txt[...]
    last = pltpu.make_async_copy(row_txt, out_txt, in_sems.at[0])
    last.start()
    for c in sent:
        c.wait()
    last.wait()


def scale_of(u):
    return lax.rsqrt(jnp.sum(u * u, axis=1, keepdims=True) + EPS)


def lse(x, axis):
    top = jnp.max(x, axis, keepdims=True)
    return top + jnp.log(jnp.sum(jnp.exp(x - top), axis, keepdims=True))


def tile_body(width, img, txt, w_img, w_txt_in, *refs):
    (row_out, col_out), outs, w_txt, made = refs[:2], refs[2:7], refs[7], refs[8:11]
    in_sems, out_sems = refs[11:]
    copies = fetch([w_txt_in], [w_txt], in_sems)
    tl_own, u_img, u_txt = made
    sources = list(made) + [img.at[:, width:], txt.at[:, width:]]
    back = [pltpu.make_async_copy(sources[k], outs[k], out_sems.at[k]) for k in range(5)]
    for c in back[3:]:
        c.start()
    tl_own[...] = TEACHER_SCALE * dot(img[:, :width], txt[:, :width], NT)
    back[0].start()
    u_img[...] = dot(img[:, width:], w_img[...])
    back[1].start()
    copies[0].wait()
    u_txt[...] = dot(txt[:, width:], w_txt[...])
    back[2].start()
    ui = u_img[...]
    ut = u_txt[...]
    ei = (ui * scale_of(ui)).astype(BF16)
    et = (ut * scale_of(ut)).astype(BF16)
    sl = STUDENT_SCALE * dot(ei, et, NT)
    tl = tl_own[...]
    es = jnp.exp(sl)
    rows, cols = tl.shape
    row_t = lse(tl, 1)
    row_s = jnp.log(jnp.sum(es, 1, keepdims=True))
    lane = lax.broadcasted_iota(jnp.int32, (rows, LANES), 1)
    turned = jnp.where(lane == 0, row_t, row_s).T
    row_out[0] = jnp.zeros((8, LANES), F32)
    for b in range(rows // LANES):
        row_out[0, 2 * b : 2 * b + 2, :] = turned[0:2, b * LANES : (b + 1) * LANES]
    rep = row_out[0]
    for k in range(1, row_out.shape[0]):
        row_out[k] = rep
    col_t = lse(tl, 0)
    col_s = jnp.log(jnp.sum(es, 0, keepdims=True))
    col_out[0] = jnp.zeros((8, LANES), F32)
    for b in range(cols // LANES):
        col_out[0, b : b + 1, :] = col_t[:, b * LANES : (b + 1) * LANES]
        col_out[0, 2 + b : 3 + b, :] = col_s[:, b * LANES : (b + 1) * LANES]
    rep = col_out[0]
    for k in range(1, col_out.shape[0]):
        col_out[k] = rep
    for c in back:
        c.wait()


def tangent(grad_rows, embeds, inverse):
    return (grad_rows - embeds * jnp.sum(embeds * grad_rows, 1, keepdims=True)) * inverse


def grad_body(core, row_all, col_all, *refs):
    ins, (keep, send, loss), held, (g, wi, wt, sems) = refs[:5], refs[5:8], refs[8:13], refs[13:]
    copies = fetch(ins, held, sems)
    tl, u_img, u_txt, feats_img, feats_txt = held
    rows, cols = tl.shape
    row_parts, col_parts = (row_all.shape[0], col_all.shape[0])
    row = lse(row_all[...], 0)[0]
    col = lse(col_all[...], 0)[0]
    sub = lax.broadcasted_iota(jnp.int32, (8, LANES), 0)
    row_term = jnp.where(sub % 2 == 1, row, -row)
    col_term = jnp.where(sub < 2, -col, jnp.where(sub < 4, col, 0.0))
    total = jnp.sum(row_term, keepdims=True) / row_parts + jnp.sum(col_term, keepdims=True) / col_parts
    down = row.T
    col_t = jnp.concatenate([col[0:1], col[1:2]], 1)
    col_s = jnp.concatenate([col[2:3], col[3:4]], 1)
    acc = jnp.zeros((LANES, cols), F32)
    for c in copies:
        c.wait()
    ui = u_img[...]
    ut = u_txt[...]
    inv_img = scale_of(ui)
    inv_txt = scale_of(ut)
    ei = ui * inv_img
    et = ut * inv_txt
    sl = STUDENT_SCALE * dot(ei.astype(BF16), et.astype(BF16), NT)
    for b in range(rows // LANES):
        at = pl.ds(b * LANES, LANES)
        t = tl[at, :]
        s = sl[b * LANES : (b + 1) * LANES]
        pt_row = jnp.exp(t - down[:, 2 * b : 2 * b + 1])
        ps_row = jnp.exp(s - down[:, 2 * b + 1 : 2 * b + 2])
        pt_col = jnp.exp(t - col_t)
        ps_col = jnp.exp(s - col_s)
        acc = acc + (pt_row + pt_col) * (t - s)
        g[at, :] = (0.5 * STUDENT_SCALE * ((ps_row - pt_row) + (ps_col - pt_col))).astype(BF16)
    total = total + jnp.sum(acc, keepdims=True)
    loss[...] = jnp.broadcast_to(total, (8, LANES))
    gb = g[...]
    di = dot(gb, et.astype(BF16))
    dt = dot(gb, ei.astype(BF16), TN)
    wi[...] = dot(feats_img[...], tangent(di, ei, inv_img).astype(BF16), TN).astype(BF16)
    wt[...] = dot(feats_txt[...], tangent(dt, et, inv_txt).astype(BF16), TN).astype(BF16)
    hi, ht = (wi.shape[0] // 2, wt.shape[0] // 2)
    me = core[0]
    for out, who in ((keep, me), (send, 1 - me)):
        a = wi[pl.ds(pl.multiple_of(who * hi, hi), hi), :]
        b = wt[pl.ds(pl.multiple_of(who * ht, ht), ht), :]
        tall, low = (TALL, CHUNK - TALL)
        for p in range(out.shape[0]):
            i, j = divmod(p, 4)
            lanes = slice(j * LANES, (j + 1) * LANES)
            out[p, :tall, :] = a[i * tall : (i + 1) * tall, lanes]
            out[p, tall:, :] = b[i * low : (i + 1) * low, lanes]


def pair_body(a, b, out):
    out[...] = (a[...].astype(F32) + b[...].astype(F32)).astype(BF16)


def thirds(value):
    hi = value.astype(BF16).astype(F32)
    mid = (value - hi).astype(BF16).astype(F32)
    low = value - hi - mid
    lane = lax.broadcasted_iota(jnp.int32, value.shape, 1)
    split = jnp.where(lane == 0, hi, jnp.where(lane == 1, mid, jnp.where(lane == 2, low, 0.0)))
    return split.astype(BF16)


def fold_body(parts, *refs):
    out = refs[-1]
    whole = jnp.sum(parts[:, :CHUNK, :].astype(F32), 0).astype(BF16)
    if len(refs) > 1:
        value = jnp.concatenate([refs[0][...]] * 2, 0)
    else:
        terms = jnp.sum(parts[:, CHUNK:, :].astype(F32), 0)
        value = jnp.broadcast_to(jnp.sum(terms, 1, keepdims=True), (BOX - CHUNK, LANES))
    split = thirds(value)
    for k in range(out.shape[0]):
        out[k, :CHUNK, :] = whole
        out[k, CHUNK:, :] = split


def output_body(scale, core, own, other, loss, grad_img, grad_txt):
    hi, ht = (grad_img.shape[0] // 2, grad_txt.shape[0] // 2)
    me = core[0]
    tall, low = (TALL, CHUNK - TALL)
    sums = []
    for box, who in ((own, me), (other, 1 - me)):
        for p in range(box.shape[0]):
            i, j = divmod(p, 4)
            lanes = slice(j * LANES, (j + 1) * LANES)
            at = pl.multiple_of(who * hi + i * tall, 8)
            grad_img[pl.ds(at, tall), lanes] = box[p, :tall, :].astype(F32)
            at = pl.multiple_of(who * ht + i * low, 8)
            grad_txt[pl.ds(at, low), lanes] = box[p, tall:CHUNK, :].astype(F32)
        terms = jnp.sum(box[:, CHUNK:, :].astype(F32), 0)
        sums.append(jnp.sum(terms[:1], keepdims=True))
    loss[...] = (sums[0] + sums[1]) * scale


def exchange(copies, axes):
    return lax.all_to_all(copies, axes, 0, 0, tiled=True)


def swap_cores(block):
    return lax.ppermute(block, "core", [(0, 1), (1, 0)])


def shards(image_feats, text_feats, teacher_img, teacher_txt, proj_img, proj_txt):
    core = lax.axis_index("core").reshape(1)
    n_tile, n_ring, n_plane = (lax.axis_size(a) for a in (TILE, RING, PLANE))
    n_near, n_far = (lax.axis_size(a) for a in (NEAR, FAR))
    own, width = teacher_img.shape
    wide_i = width + image_feats.shape[1]
    wide_t = width + text_feats.shape[1]
    rows, cols = (own * n_tile, own * n_ring)
    depth = proj_img.shape[1]

    raw = (teacher_img, image_feats, teacher_txt, text_feats)
    pack_img, pack_txt = pl.pallas_call(
        pack_body,
        out_shape=[pltpu.HBM((n_tile, own, wide_i), BF16), pltpu.HBM((own, wide_t), BF16)],
        in_specs=[HBM] * 4,
        out_specs=[HBM] * 2,
        scratch_shapes=[pltpu.VMEM(a.shape, a.dtype) for a in raw]
        + [
            pltpu.VMEM((own, wide_i), BF16),
            pltpu.VMEM((own, wide_t), BF16),
            pltpu.SemaphoreType.DMA((4,)),
            pltpu.SemaphoreType.DMA((n_tile,)),
        ],
        compiler_params=room(8),
    )(*[pinned(a) for a in raw])
    pack_img, core = lax.optimization_barrier((pack_img, core))
    img = exchange(pack_img, TILE).reshape(rows, wide_i)
    txt = lax.all_gather(pack_txt, RING, axis=0, tiled=True)

    blocks = [(rows, cols), (rows, depth), (cols, depth)]
    feats = [(rows, proj_img.shape[0]), (cols, proj_txt.shape[0])]
    row_part, col_part, *kept = pl.pallas_call(
        functools.partial(tile_body, width),
        out_shape=[jax.ShapeDtypeStruct((n, 8, LANES), F32) for n in (n_tile, n_ring)]
        + [pltpu.HBM(b, F32) for b in blocks]
        + [pltpu.HBM(b, BF16) for b in feats],
        in_specs=[VMEM] * 3 + [HBM],
        out_specs=[VMEM] * 2 + [HBM] * 5,
        scratch_shapes=[pltpu.VMEM(proj_txt.shape, BF16)]
        + [pltpu.VMEM(b, F32) for b in blocks]
        + [pltpu.SemaphoreType.DMA((n,)) for n in (1, 5)],
        compiler_params=room(24),
    )(img, txt, proj_img, pinned(proj_txt))
    row_all = exchange(row_part, TILE)
    col_part, row_all = lax.optimization_barrier((col_part, row_all))
    col_all = exchange(col_part, RING)

    box = (n_plane, CHUNK, LANES)
    keep, send, total = pl.pallas_call(
        grad_body,
        out_shape=[
            jax.ShapeDtypeStruct(box, BF16),
            jax.ShapeDtypeStruct(box, BF16),
            jax.ShapeDtypeStruct((8, LANES), F32),
        ],
        in_specs=[SMEM, VMEM, VMEM] + [HBM] * 5,
        out_specs=[VMEM] * 3,
        scratch_shapes=[pltpu.VMEM(b, F32) for b in blocks]
        + [
            pltpu.VMEM(feats[0], BF16),
            pltpu.VMEM(feats[1], BF16),
            pltpu.VMEM((rows, cols), BF16),
            pltpu.VMEM(proj_img.shape, BF16),
            pltpu.VMEM(proj_txt.shape, BF16),
            pltpu.SemaphoreType.DMA((5,)),
        ],
        compiler_params=room(24),
    )(core, row_all, col_all, *[pinned(k) for k in kept])

    (part,) = call(pair_body, 8, [(box, BF16)], keep, swap_cores(send))
    part = exchange(part, PLANE)
    (part,) = call(fold_body, 8, [((n_near, BOX, LANES), BF16)], part, total)
    part = exchange(part, NEAR)
    (part,) = call(fold_body, 8, [((1, BOX, LANES), BF16)], part)
    part = lax.all_gather(part, FAR, axis=0, tiled=True)
    (part,) = call(fold_body, 8, [((n_plane, BOX, LANES), BF16)], part)
    mine = exchange(part, PLANE)
    other = swap_cores(mine)
    batch_total = own * lax.axis_size(AXES)
    loss, grad_img, grad_txt = call(
        functools.partial(output_body, 1.0 / (2.0 * batch_total)),
        10,
        [((1, 1), F32), (proj_img.shape, F32), (proj_txt.shape, F32)],
        core,
        mine,
        other,
        scalars=1,
    )
    return (loss.reshape(()), grad_img, grad_txt)


def solution(mesh):
    fine = Mesh(mesh.devices.reshape(SIZES), AXES)
    img = P(("zm", "zn", "core", "y", "zh", "x"), None)
    txt = P(("y", "zh", "x", "zm", "zn", "core"), None)
    return jax.shard_map(
        shards,
        mesh=fine,
        in_specs=(img, txt, img, txt, P(), P()),
        out_specs=(P(), P(), P()),
        check_vma=False,
    )
```

```python
import functools

import jax
import jax.numpy as jnp
from jax import lax
from jax.experimental import pallas as pl
from jax.experimental.pallas import tpu as pltpu
from jax.sharding import Mesh
from jax.sharding import PartitionSpec as P

EPS = 1e-06
TEACHER_SCALE = 100.0
STUDENT_SCALE = 50.0

AXES = ("zm", "zn", "core", "y", "zh", "x")
SIZES = (2, 4, 2, 4, 2, 4)
PLANE = ("y", "x")
NEAR = ("zn",)
FAR = ("zh", "zm")
RING = FAR + NEAR
TILE = ("y", "x", "core")

BF16 = jnp.bfloat16
F32 = jnp.float32
LANES = 128
TALL = 96
CHUNK = 160
BOX = 176

NT = (((1,), (1,)), ((), ()))
TN = (((0,), (0,)), ((), ()))


def room(mib):
    return pltpu.CompilerParams(vmem_limit_bytes=mib * 1024 * 1024)


def call(body, mib, outs, *args, scalars=0):
    vmem = pl.BlockSpec(memory_space=pltpu.VMEM)
    smem = pl.BlockSpec(memory_space=pltpu.SMEM)
    specs = [smem] * scalars + [vmem] * (len(args) - scalars)
    shapes = [jax.ShapeDtypeStruct(s, t) for s, t in outs]
    return pl.pallas_call(
        body,
        out_shape=shapes,
        in_specs=specs,
        out_specs=[vmem] * len(outs),
        compiler_params=room(mib),
    )(*args)


def fetch(sources, held, sems):
    copies = [pltpu.make_async_copy(a, b, sems.at[k]) for k, (a, b) in enumerate(zip(sources, held))]
    for c in copies:
        c.start()
    return copies


def pinned(array):
    return pltpu.with_memory_space_constraint(array, pltpu.HBM)


HBM = pl.BlockSpec(memory_space=pltpu.HBM)
VMEM = pl.BlockSpec(memory_space=pltpu.VMEM)
SMEM = pl.BlockSpec(memory_space=pltpu.SMEM)


def dot(a, b, dims=(((1,), (0,)), ((), ()))):
    return lax.dot_general(a, b, dims, preferred_element_type=F32)


def normed(raw):
    x = raw.astype(F32)
    return (x * lax.rsqrt(jnp.sum(x * x, axis=1, keepdims=True) + EPS)).astype(BF16)


def pack_body(*refs):
    ins, (out_img, out_txt), held = refs[:4], refs[4:6], refs[6:10]
    row_img, row_txt, in_sems, out_sems = refs[10:]
    copies = fetch(ins, held, in_sems)
    teach_img, feats_img, teach_txt, feats_txt = held
    width = teach_img.shape[1]
    copies[0].wait()
    copies[1].wait()
    row_img[:, :width] = normed(teach_img[...])
    row_img[:, width:] = feats_img[...]
    peers = out_img.shape[0]
    sent = fetch([row_img] * peers, [out_img.at[k] for k in range(peers)], out_sems)
    copies[2].wait()
    copies[3].wait()
    row_txt[:, :width] = normed(teach_txt[...])
    row_txt[:, width:] = feats_txt[...]
    last = pltpu.make_async_copy(row_txt, out_txt, in_sems.at[0])
    last.start()
    for c in sent:
        c.wait()
    last.wait()


def scale_of(u):
    return lax.rsqrt(jnp.sum(u * u, axis=1, keepdims=True) + EPS)


def lse(x, axis):
    top = jnp.max(x, axis, keepdims=True)
    return top + jnp.log(jnp.sum(jnp.exp(x - top), axis, keepdims=True))


def tile_body(width, img, txt, w_img, w_txt_in, *refs):
    (row_out, col_out), outs, w_txt, made = refs[:2], refs[2:8], refs[8], refs[9:13]
    in_sems, out_sems = refs[13:]
    copies = fetch([w_txt_in], [w_txt], in_sems)
    tl_own, sl_own, u_img, u_txt = made
    sources = list(made) + [img.at[:, width:], txt.at[:, width:]]
    back = [pltpu.make_async_copy(sources[k], outs[k], out_sems.at[k]) for k in range(6)]
    back[4].start()
    back[5].start()
    tl_own[...] = TEACHER_SCALE * dot(img[:, :width], txt[:, :width], NT)
    back[0].start()
    u_img[...] = dot(img[:, width:], w_img[...])
    back[2].start()
    copies[0].wait()
    u_txt[...] = dot(txt[:, width:], w_txt[...])
    back[3].start()
    ui = u_img[...]
    ut = u_txt[...]
    ei = (ui * scale_of(ui)).astype(BF16)
    et = (ut * scale_of(ut)).astype(BF16)
    sl_own[...] = STUDENT_SCALE * dot(ei, et, NT)
    back[1].start()
    tl = tl_own[...]
    sl = sl_own[...]
    es = jnp.exp(sl)
    rows, cols = tl.shape
    row_t = lse(tl, 1)
    row_s = jnp.log(jnp.sum(es, 1, keepdims=True))
    lane = lax.broadcasted_iota(jnp.int32, (rows, LANES), 1)
    turned = jnp.where(lane == 0, row_t, row_s).T
    row_out[0] = jnp.zeros((8, LANES), F32)
    for b in range(rows // LANES):
        row_out[0, 2 * b : 2 * b + 2, :] = turned[0:2, b * LANES : (b + 1) * LANES]
    rep = row_out[0]
    for k in range(1, row_out.shape[0]):
        row_out[k] = rep
    col_t = lse(tl, 0)
    col_s = jnp.log(jnp.sum(es, 0, keepdims=True))
    col_out[0] = jnp.zeros((8, LANES), F32)
    for b in range(cols // LANES):
        col_out[0, b : b + 1, :] = col_t[:, b * LANES : (b + 1) * LANES]
        col_out[0, 2 + b : 3 + b, :] = col_s[:, b * LANES : (b + 1) * LANES]
    rep = col_out[0]
    for k in range(1, col_out.shape[0]):
        col_out[k] = rep
    for c in back:
        c.wait()


def tangent(grad_rows, embeds, inverse):
    return (grad_rows - embeds * jnp.sum(embeds * grad_rows, 1, keepdims=True)) * inverse


def grad_body(core, row_all, col_all, *refs):
    ins, (keep, send, loss), held, (g, wi, wt, sems) = refs[:6], refs[6:9], refs[9:15], refs[15:]
    copies = fetch(ins, held, sems)
    tl, sl, u_img, u_txt, feats_img, feats_txt = held
    rows, cols = tl.shape
    row_parts, col_parts = (row_all.shape[0], col_all.shape[0])
    row = lse(row_all[...], 0)[0]
    col = lse(col_all[...], 0)[0]
    sub = lax.broadcasted_iota(jnp.int32, (8, LANES), 0)
    row_term = jnp.where(sub % 2 == 1, row, -row)
    col_term = jnp.where(sub < 2, -col, jnp.where(sub < 4, col, 0.0))
    total = jnp.sum(row_term, keepdims=True) / row_parts + jnp.sum(col_term, keepdims=True) / col_parts
    down = row.T
    col_t = jnp.concatenate([col[0:1], col[1:2]], 1)
    col_s = jnp.concatenate([col[2:3], col[3:4]], 1)
    acc = jnp.zeros((LANES, cols), F32)
    copies[0].wait()
    copies[1].wait()
    for b in range(rows // LANES):
        at = pl.ds(b * LANES, LANES)
        t = tl[at, :]
        s = sl[at, :]
        pt_row = jnp.exp(t - down[:, 2 * b : 2 * b + 1])
        ps_row = jnp.exp(s - down[:, 2 * b + 1 : 2 * b + 2])
        pt_col = jnp.exp(t - col_t)
        ps_col = jnp.exp(s - col_s)
        acc = acc + (pt_row + pt_col) * (t - s)
        g[at, :] = (0.5 * STUDENT_SCALE * ((ps_row - pt_row) + (ps_col - pt_col))).astype(BF16)
    total = total + jnp.sum(acc, keepdims=True)
    loss[...] = jnp.broadcast_to(total, (8, LANES))
    for c in copies[2:]:
        c.wait()
    ui = u_img[...]
    ut = u_txt[...]
    inv_img = scale_of(ui)
    inv_txt = scale_of(ut)
    ei = ui * inv_img
    et = ut * inv_txt
    gb = g[...]
    di = dot(gb, et.astype(BF16))
    dt = dot(gb, ei.astype(BF16), TN)
    wi[...] = dot(feats_img[...], tangent(di, ei, inv_img).astype(BF16), TN).astype(BF16)
    wt[...] = dot(feats_txt[...], tangent(dt, et, inv_txt).astype(BF16), TN).astype(BF16)
    hi, ht = (wi.shape[0] // 2, wt.shape[0] // 2)
    me = core[0]
    for out, who in ((keep, me), (send, 1 - me)):
        a = wi[pl.ds(pl.multiple_of(who * hi, hi), hi), :]
        b = wt[pl.ds(pl.multiple_of(who * ht, ht), ht), :]
        tall, low = (TALL, CHUNK - TALL)
        for p in range(out.shape[0]):
            i, j = divmod(p, 4)
            lanes = slice(j * LANES, (j + 1) * LANES)
            out[p, :tall, :] = a[i * tall : (i + 1) * tall, lanes]
            out[p, tall:, :] = b[i * low : (i + 1) * low, lanes]


def pair_body(a, b, out):
    out[...] = (a[...].astype(F32) + b[...].astype(F32)).astype(BF16)


def thirds(value):
    hi = value.astype(BF16).astype(F32)
    mid = (value - hi).astype(BF16).astype(F32)
    low = value - hi - mid
    lane = lax.broadcasted_iota(jnp.int32, value.shape, 1)
    split = jnp.where(lane == 0, hi, jnp.where(lane == 1, mid, jnp.where(lane == 2, low, 0.0)))
    return split.astype(BF16)


def fold_body(parts, *refs):
    out = refs[-1]
    whole = jnp.sum(parts[:, :CHUNK, :].astype(F32), 0).astype(BF16)
    if len(refs) > 1:
        value = jnp.concatenate([refs[0][...]] * 2, 0)
    else:
        terms = jnp.sum(parts[:, CHUNK:, :].astype(F32), 0)
        value = jnp.broadcast_to(jnp.sum(terms, 1, keepdims=True), (BOX - CHUNK, LANES))
    split = thirds(value)
    for k in range(out.shape[0]):
        out[k, :CHUNK, :] = whole
        out[k, CHUNK:, :] = split


def output_body(scale, core, own, other, loss, grad_img, grad_txt):
    hi, ht = (grad_img.shape[0] // 2, grad_txt.shape[0] // 2)
    me = core[0]
    tall, low = (TALL, CHUNK - TALL)
    sums = []
    for box, who in ((own, me), (other, 1 - me)):
        for p in range(box.shape[0]):
            i, j = divmod(p, 4)
            lanes = slice(j * LANES, (j + 1) * LANES)
            at = pl.multiple_of(who * hi + i * tall, 8)
            grad_img[pl.ds(at, tall), lanes] = box[p, :tall, :].astype(F32)
            at = pl.multiple_of(who * ht + i * low, 8)
            grad_txt[pl.ds(at, low), lanes] = box[p, tall:CHUNK, :].astype(F32)
        terms = jnp.sum(box[:, CHUNK:, :].astype(F32), 0)
        sums.append(jnp.sum(terms[:1], keepdims=True))
    loss[...] = (sums[0] + sums[1]) * scale


def exchange(copies, axes):
    return lax.all_to_all(copies, axes, 0, 0, tiled=True)


def swap_cores(block):
    return lax.ppermute(block, "core", [(0, 1), (1, 0)])


def shards(image_feats, text_feats, teacher_img, teacher_txt, proj_img, proj_txt):
    core = lax.axis_index("core").reshape(1)
    n_tile, n_ring, n_plane = (lax.axis_size(a) for a in (TILE, RING, PLANE))
    n_near, n_far = (lax.axis_size(a) for a in (NEAR, FAR))
    own, width = teacher_img.shape
    wide_i = width + image_feats.shape[1]
    wide_t = width + text_feats.shape[1]
    rows, cols = (own * n_tile, own * n_ring)
    depth = proj_img.shape[1]

    raw = (teacher_img, image_feats, teacher_txt, text_feats)
    pack_img, pack_txt = pl.pallas_call(
        pack_body,
        out_shape=[pltpu.HBM((n_tile, own, wide_i), BF16), pltpu.HBM((own, wide_t), BF16)],
        in_specs=[HBM] * 4,
        out_specs=[HBM] * 2,
        scratch_shapes=[pltpu.VMEM(a.shape, a.dtype) for a in raw]
        + [
            pltpu.VMEM((own, wide_i), BF16),
            pltpu.VMEM((own, wide_t), BF16),
            pltpu.SemaphoreType.DMA((4,)),
            pltpu.SemaphoreType.DMA((n_tile,)),
        ],
        compiler_params=room(8),
    )(*[pinned(a) for a in raw])
    pack_img, core = lax.optimization_barrier((pack_img, core))
    img = exchange(pack_img, TILE).reshape(rows, wide_i)
    txt = lax.all_gather(pack_txt, RING, axis=0, tiled=True)

    blocks = [(rows, cols), (rows, cols), (rows, depth), (cols, depth)]
    feats = [(rows, proj_img.shape[0]), (cols, proj_txt.shape[0])]
    row_part, col_part, *kept = pl.pallas_call(
        functools.partial(tile_body, width),
        out_shape=[jax.ShapeDtypeStruct((n, 8, LANES), F32) for n in (n_tile, n_ring)]
        + [pltpu.HBM(b, F32) for b in blocks]
        + [pltpu.HBM(b, BF16) for b in feats],
        in_specs=[VMEM] * 3 + [HBM],
        out_specs=[VMEM] * 2 + [HBM] * 6,
        scratch_shapes=[pltpu.VMEM(proj_txt.shape, BF16)]
        + [pltpu.VMEM(b, F32) for b in blocks]
        + [pltpu.SemaphoreType.DMA((n,)) for n in (1, 6)],
        compiler_params=room(24),
    )(img, txt, proj_img, pinned(proj_txt))
    row_all = exchange(row_part, TILE)
    col_part, row_all = lax.optimization_barrier((col_part, row_all))
    col_all = exchange(col_part, RING)

    box = (n_plane, CHUNK, LANES)
    keep, send, total = pl.pallas_call(
        grad_body,
        out_shape=[
            jax.ShapeDtypeStruct(box, BF16),
            jax.ShapeDtypeStruct(box, BF16),
            jax.ShapeDtypeStruct((8, LANES), F32),
        ],
        in_specs=[SMEM, VMEM, VMEM] + [HBM] * 6,
        out_specs=[VMEM] * 3,
        scratch_shapes=[pltpu.VMEM(b, F32) for b in blocks]
        + [
            pltpu.VMEM(feats[0], BF16),
            pltpu.VMEM(feats[1], BF16),
            pltpu.VMEM((rows, cols), BF16),
            pltpu.VMEM(proj_img.shape, BF16),
            pltpu.VMEM(proj_txt.shape, BF16),
            pltpu.SemaphoreType.DMA((6,)),
        ],
        compiler_params=room(24),
    )(core, row_all, col_all, *[pinned(k) for k in kept])

    (part,) = call(pair_body, 8, [(box, BF16)], keep, swap_cores(send))
    part = exchange(part, PLANE)
    (part,) = call(fold_body, 8, [((n_near, BOX, LANES), BF16)], part, total)
    part = exchange(part, NEAR)
    (part,) = call(fold_body, 8, [((1, BOX, LANES), BF16)], part)
    part = lax.all_gather(part, FAR, axis=0, tiled=True)
    (part,) = call(fold_body, 8, [((n_plane, BOX, LANES), BF16)], part)
    mine = exchange(part, PLANE)
    other = swap_cores(mine)
    batch_total = own * lax.axis_size(AXES)
    loss, grad_img, grad_txt = call(
        functools.partial(output_body, 1.0 / (2.0 * batch_total)),
        10,
        [((1, 1), F32), (proj_img.shape, F32), (proj_txt.shape, F32)],
        core,
        mine,
        other,
        scalars=1,
    )
    return (loss.reshape(()), grad_img, grad_txt)


def solution(mesh):
    fine = Mesh(mesh.devices.reshape(SIZES), AXES)
    img = P(("zm", "zn", "core", "y", "zh", "x"), None)
    txt = P(("y", "zh", "x", "zm", "zn", "core"), None)
    return jax.shard_map(
        shards,
        mesh=fine,
        in_specs=(img, txt, img, txt, P(), P()),
        out_specs=(P(), P(), P()),
        check_vma=False,
    )
```
